32 devices in a mesh: group: 2 (over x), tensor: 8 (over z, y), adapter: 2 (over core).
Axes of the slice: x: 2, y: 2, z: 4, core: 2. Of those that a mesh axis runs over, the one named last changes fastest.
Arguments:
- hidden: bfloat16 [2, 256, 8192], P('adapter', 'group', 'tensor'), parts along dimension 1, may hold values from -6 to 6
- input_norm_scale: float32 [8192], replicated, may hold values from 0.5 to 1.5
- query_weight: bfloat16 [8192, 8192], P(None, 'tensor'), may hold values from -0.0625 to 0.0625
- key_value_weight: bfloat16 [8192, 2048], P('tensor'), may hold values from -0.0625 to 0.0625
- adapter_down_weight: bfloat16 [8, 8192, 192], P(('group', 'adapter'), 'tensor'), parts along dimension 0, may hold values from -0.0625 to 0.0625
- adapter_up_query: bfloat16 [8, 64, 8192], P(('group', 'adapter'), None, 'tensor'), parts along dimension 0, may hold values from -0.75 to 0.75
- adapter_up_key_value: bfloat16 [8, 2, 64, 1024], P(('group', 'adapter')), parts along dimension 0, may hold values from -0.75 to 0.75
- request_adapter: int32 [2, 256], P('adapter', 'group'), parts along dimension 1, may hold values from 0 to 3, never falling along the last dimension, each value on 1 to 64 neighbouring positions
- key_value_cache: bfloat16 [2, 256, 2, 96, 1024], P('adapter', ('group', 'tensor')), parts along dimension 1, may hold values from -240 to 240
- lengths: int32 [2, 256], P('adapter', ('group', 'tensor')), parts along dimension 1, may hold values from 1 to 96, 6144 in all within a row
Outputs:
- attended: bfloat16 [2, 256, 8192], P('adapter', ('group', 'tensor')), parts along dimension 1
- new_kv: bfloat16 [2, 256, 2, 1024], P('adapter', ('group', 'tensor')), parts along dimension 1
The draws below stay inside these ranges and needn't reach their ends.
There are 2 independent parts, one for each index of `group`. The reference program is written for one: setup_inputs(seed, part) draws one part's arguments, and reference() takes and returns one part's arrays. A program takes and returns all parts, laid end to end along the dimension named above; an argument that names none is the same for every part. Nothing has to cross between parts.
Inputs may be any that keep to these rules, and one draw needn't show every extreme that they name: `request_adapter`: within each batch the ids never fall; every adapter has 1 to 64 rows of the batch and one has exactly 64. `lengths`: in each batch some row has exactly 96.
All inputs are finite; a program needn't handle non-finite values. No bound on the sum of `lengths` on one device may be relied on, other than what follows from the above.
Results may differ from the reference program's by a relative error of at most 0.0065.
The reference program's roundings to bfloat16 on the way (of `normed`, `shrink_low`, `q_raw`, `q_rot` and `weights`) count: a program that leaves them out, or rounds other values in their place, can miss the bound.
Values may be sent and summed in bfloat16 or wider, within the bound.
No kernel may reach another device: no remote copies, remote signals or barrier semaphores. Data moves between devices by JAX's collectives and lax.ppermute only.
A program may use at most 128 MiB of HBM per device.

```python
import math
import jax
import jax.numpy as jnp
import numpy as np
from jax import lax

MODEL_WIDTH = 8192
QUERY_HEADS = 64
KEY_HEADS = 8
HEAD_WIDTH = 128
ADAPTER_RANK = 64
CACHE_LENGTH = 96
BATCH_ROWS = 128
ADAPTER_COUNT = 4
BATCH_COUNT = 2


def draw_key_value_cache(key, part):
    key = jax.random.fold_in(key, 7)
    random_key_value = jax.random.fold_in(key, 0)
    value_rows = jnp.clip(jax.random.normal(random_key_value, (BATCH_COUNT, BATCH_ROWS, 2, CACHE_LENGTH, KEY_HEADS * HEAD_WIDTH), jnp.float32), -6.0, 6.0)
    return value_rows.astype(jnp.bfloat16)


def levels(rng, extent, cuts, least, top_value):
    gain = 1.0
    for axis_at, shards_of in cuts:
        heights = jax.random.uniform(jax.random.fold_in(jax.random.fold_in(rng, 6), axis_at), (shards_of,), jnp.float32, least / len(cuts), top_value / len(cuts))
        gain = gain * jnp.repeat(jnp.exp(heights), extent[axis_at] // shards_of).reshape((-1,) + (1,) * (len(extent) - 1 - axis_at))
    return gain


def length_profile(count, total, reach, lean):
    weights = [(1 << 20) // math.isqrt(grade ** lean) + 1 for grade in range(2, count + 1)]
    rest, given = total - reach - (count - 1), [1] * (count - 1)
    while rest > 0:
        candidates = [i for i in range(count - 1) if given[i] < reach]
        whole, left = sum([weights[i] for i in candidates]), rest
        for i in candidates:
            more = min(reach - given[i], max(1, left * weights[i] // whole), rest)
            given[i] = given[i] + more
            rest = rest - more
    return np.array([reach] + given)


def uneven_parts(key, amount, total, limit, lean):
    if amount == 2:
        one = jax.random.randint(key, (), max(1, total - limit), min(limit, total - 1) + 1)
        return jnp.stack([one, total - one])
    sizes = jnp.asarray(length_profile(amount, total, limit, lean), jnp.int32)
    couples = (amount - 1) // 2
    giver, receiver = sizes[1:1 + 2 * couples:2], sizes[2:2 + 2 * couples:2]
    room = jnp.minimum(giver - 1, limit - receiver)
    shifted = jax.random.randint(jax.random.fold_in(key, 1), (couples,), 0, 1 << 20) % (room + 1)
    sizes = sizes.at[1:1 + 2 * couples:2].set(giver - shifted).at[2:2 + 2 * couples:2].set(receiver + shifted)
    return sizes[jax.random.permutation(jax.random.fold_in(key, 2), amount)]


def centred(stream_key, extent, width, most, shards=(), dtype=jnp.bfloat16):
    entries = jax.random.normal(stream_key, extent, jnp.float32) * width
    if len(shards) > 0:
        entries = levels(stream_key, extent, shards, -0.22, 0.18) * entries
    return jnp.clip(entries, min=-most, max=most).astype(dtype)


def setup_inputs(seed: int = 0, part: int = 0) -> dict:
    key_of = jax.random.split(jax.random.key(seed), 11)
    own_keys = jax.random.split(jax.random.fold_in(key_of[10], part), 11)
    return {
        "hidden": centred(own_keys[0], (BATCH_COUNT, BATCH_ROWS, MODEL_WIDTH), 1.0, 6.0, ((0, 2), (2, 8))),
        "input_norm_scale": jnp.clip(1.0 + 0.1 * jax.random.normal(key_of[1], (MODEL_WIDTH,), jnp.float32), 0.5, 1.5),
        "query_weight": centred(key_of[2], (MODEL_WIDTH, QUERY_HEADS * HEAD_WIDTH), MODEL_WIDTH ** -0.5, 0.0625, ((1, 8),)),
        "key_value_weight": centred(key_of[3], (MODEL_WIDTH, 2 * KEY_HEADS * HEAD_WIDTH), MODEL_WIDTH ** -0.5, 0.0625, ((0, 8),)),
        "adapter_down_weight": centred(own_keys[4], (ADAPTER_COUNT, MODEL_WIDTH, 3 * ADAPTER_RANK), MODEL_WIDTH ** -0.5, 0.0625, ((0, 2), (1, 8))),
        "adapter_up_query": centred(own_keys[5], (ADAPTER_COUNT, ADAPTER_RANK, QUERY_HEADS * HEAD_WIDTH), ADAPTER_RANK ** -0.5, 0.75, ((0, 2), (2, 8))),
        "adapter_up_key_value": centred(own_keys[6], (ADAPTER_COUNT, 2, ADAPTER_RANK, KEY_HEADS * HEAD_WIDTH), ADAPTER_RANK ** -0.5, 0.75, ((0, 2),)),
        "request_adapter": jax.vmap(lambda own: jnp.searchsorted(jnp.cumsum(uneven_parts(own, ADAPTER_COUNT, BATCH_ROWS, BATCH_ROWS // 2, 2)), jnp.arange(BATCH_ROWS), side="right"))(jax.random.split(own_keys[7], BATCH_COUNT)).reshape((BATCH_COUNT, BATCH_ROWS)).astype(jnp.int32),
        "key_value_cache": draw_key_value_cache(jax.random.fold_in(jax.random.fold_in(key_of[10], part), 71), part),
        "lengths": jax.vmap(lambda own: uneven_parts(own, BATCH_ROWS, BATCH_ROWS * CACHE_LENGTH // 2, CACHE_LENGTH, 2))(jax.random.split(own_keys[9], BATCH_COUNT)).reshape((BATCH_COUNT, BATCH_ROWS)).astype(jnp.int32),
    }


EPS = 1e-05
THETA = 500000.0

def apply_rotary(value_rows, token_positions, heads):
    request_row_count = value_rows.shape[0]
    shaped = value_rows.reshape(request_row_count, heads, HEAD_WIDTH)
    half_dim = HEAD_WIDTH // 2
    frequency = THETA ** (-(jnp.arange(half_dim).astype(jnp.float32) * 2.0 / HEAD_WIDTH))
    angles = token_positions.astype(jnp.float32)[:, None] * frequency[None, :]
    cosine = jnp.cos(angles)[:, None, :]
    sine_values = jnp.sin(angles)[:, None, :]
    leading = shaped[..., :half_dim]
    second = shaped[..., half_dim:]
    turned = jnp.concatenate([leading * cosine - second * sine_values, second * cosine + leading * sine_values], axis=-1)
    return turned.reshape(request_row_count, heads * HEAD_WIDTH)

def attend(query_vector, newest_token, layer_cache, request_lengths):
    request_row_count = query_vector.shape[0]
    query_group_width = QUERY_HEADS // KEY_HEADS
    token_positions = layer_cache.shape[2]
    score_scale = 1.0 / math.sqrt(HEAD_WIDTH)
    query_head_rows = query_vector.astype(jnp.float32).reshape(request_row_count, KEY_HEADS, query_group_width, HEAD_WIDTH)
    cached_key_rows = layer_cache[:, 0].astype(jnp.float32).reshape(request_row_count, token_positions, KEY_HEADS, HEAD_WIDTH)
    cached_value_rows = layer_cache[:, 1].astype(jnp.float32).reshape(request_row_count, token_positions, KEY_HEADS, HEAD_WIDTH)
    newest_key = newest_token[:, 0].astype(jnp.float32).reshape(request_row_count, KEY_HEADS, HEAD_WIDTH)
    newest_value = newest_token[:, 1].astype(jnp.float32).reshape(request_row_count, KEY_HEADS, HEAD_WIDTH)
    scores = jnp.einsum('rkgd,rpkd->rkgp', query_head_rows, cached_key_rows) * score_scale
    visible = jnp.arange(token_positions)[None, :] < request_lengths[:, None]
    scores = jnp.where(visible[:, None, None, :], scores, jnp.float32(-1e+30))
    new_score = jnp.einsum('rkgd,rkd->rkg', query_head_rows, newest_key) * score_scale
    top_score = jnp.maximum(lax.optimization_barrier(jnp.max(scores, axis=-1)), new_score)
    weights = jnp.exp(scores - top_score[..., None])
    new_weight = jnp.exp(new_score - top_score)
    denominator = lax.optimization_barrier(jnp.sum(weights, axis=-1)) + new_weight
    cache_weights = (weights / denominator[..., None]).astype(jnp.bfloat16)
    fresh_weights = (new_weight / denominator).astype(jnp.bfloat16)
    mixed = jnp.einsum('rkgp,rpkd->rkgd', cache_weights.astype(jnp.float32), cached_value_rows)
    mixed = mixed + fresh_weights.astype(jnp.float32)[..., None] * newest_value[:, :, None, :]
    return mixed.reshape(request_row_count, QUERY_HEADS * HEAD_WIDTH).astype(jnp.bfloat16)

def single_batch(hidden_state_rows, request_row_index, layer_cache, request_lengths, input_norm_scale, query_weight, key_value_weight, adapter_down_weight, adapter_up_query, adapter_up_key_value):
    wide = hidden_state_rows.astype(jnp.float32)
    inverse = lax.rsqrt(lax.optimization_barrier(jnp.sum(wide * wide, axis=1)) / MODEL_WIDTH + EPS)
    normed = (wide * inverse[:, None] * input_norm_scale[None, :]).astype(jnp.bfloat16)
    q_base = jnp.dot(normed, query_weight, preferred_element_type=jnp.float32)
    kv_base = jnp.dot(normed, key_value_weight, preferred_element_type=jnp.float32)

    def shrink_step(running, adapter_number):
        selected = (request_row_index == adapter_number).astype(jnp.float32)[:, None]
        adapter_panel = lax.dynamic_index_in_dim(adapter_down_weight, adapter_number, 0, keepdims=False)
        return (running + selected * jnp.dot(normed, adapter_panel, preferred_element_type=jnp.float32), None)
    shrink, _ = lax.scan(shrink_step, jnp.zeros((BATCH_ROWS, 3 * ADAPTER_RANK), jnp.float32), jnp.arange(ADAPTER_COUNT).astype(jnp.int32))
    shrink_low = shrink.astype(jnp.bfloat16)

    def expand_step(running, adapter_number):
        selected = (request_row_index == adapter_number).astype(jnp.float32)[:, None]
        query_up_panel = lax.dynamic_index_in_dim(adapter_up_query, adapter_number, 0, keepdims=False)
        key_value_up = lax.dynamic_index_in_dim(adapter_up_key_value, adapter_number, 0, keepdims=False)
        query_delta = jnp.dot(shrink_low[:, :ADAPTER_RANK], query_up_panel, preferred_element_type=jnp.float32)
        key_delta = jnp.dot(shrink_low[:, ADAPTER_RANK:2 * ADAPTER_RANK], key_value_up[0], preferred_element_type=jnp.float32)
        value_delta = jnp.dot(shrink_low[:, 2 * ADAPTER_RANK:], key_value_up[1], preferred_element_type=jnp.float32)
        pair_delta = jnp.concatenate([key_delta, value_delta], axis=1)
        return ((running[0] + selected * query_delta, running[1] + selected * pair_delta), None)
    key_value_start = (jnp.zeros((BATCH_ROWS, QUERY_HEADS * HEAD_WIDTH), jnp.float32), jnp.zeros((BATCH_ROWS, 2 * KEY_HEADS * HEAD_WIDTH), jnp.float32))
    deltas, _ = lax.scan(expand_step, key_value_start, jnp.arange(ADAPTER_COUNT).astype(jnp.int32))
    q_raw = (q_base + deltas[0]).astype(jnp.bfloat16)
    key_value_complete = kv_base + deltas[1]
    key_spun = apply_rotary(key_value_complete[:, :KEY_HEADS * HEAD_WIDTH], request_lengths, KEY_HEADS)
    newest_token = jnp.stack([key_spun, key_value_complete[:, KEY_HEADS * HEAD_WIDTH:]], axis=1).astype(jnp.bfloat16)
    q_rot = apply_rotary(q_raw.astype(jnp.float32), request_lengths, QUERY_HEADS).astype(jnp.bfloat16)
    return (attend(q_rot, newest_token, layer_cache, request_lengths), newest_token)

def reference(hidden, input_norm_scale, query_weight, key_value_weight, adapter_down_weight, adapter_up_query, adapter_up_key_value, request_adapter, key_value_cache, lengths):
    outputs = []
    fresh_list = []
    for batch_index in range(BATCH_COUNT):
        attention_rows, newest_rows = single_batch(hidden[batch_index], request_adapter[batch_index], key_value_cache[batch_index], lengths[batch_index], input_norm_scale, query_weight, key_value_weight, adapter_down_weight, adapter_up_query, adapter_up_key_value)
        outputs.append(attention_rows)
        fresh_list.append(newest_rows)
    return (jnp.stack(outputs, axis=0), jnp.stack(fresh_list, axis=0))
```

```python
import functools
import math

import jax
import jax.numpy as jnp
import numpy as np
from jax import lax
from jax.experimental import pallas as pl
from jax.experimental.pallas import tpu as pltpu
from jax.sharding import PartitionSpec as P

HEAD_WIDTH = 128
LANES = 128
EPS = 1e-05
THETA = 500000.0
F32 = jnp.float32
BF16 = jnp.bfloat16
VMEM_LIMIT = 48 * 1024 * 1024


def ring_order(size):
    if size == 8:
        return [0, 2, 4, 6, 7, 5, 3, 1]
    return list(range(size))


def dot(a, b):
    return jnp.dot(a, b, preferred_element_type=F32)


def params(**more):
    return pltpu.CompilerParams(vmem_limit_bytes=VMEM_LIMIT, **more)


def after(value, *others):
    return lax.optimization_barrier((value, *others))[0]


def whole(shape):
    return pl.BlockSpec(shape, lambda *_: (0,) * len(shape))


def rotary_tables(positions):
    half = HEAD_WIDTH // 2
    frequency = THETA ** (-(jnp.arange(half).astype(F32) * 2.0 / HEAD_WIDTH))
    angles = positions.astype(F32)[:, None] * frequency[None, :]
    cosine = jnp.cos(angles)
    sine = jnp.sin(angles)
    return jnp.concatenate([cosine, cosine], axis=1), jnp.concatenate([-sine, sine], axis=1)


def rotate_heads(values, cosine, sine):
    turned = []
    for head in range(values.shape[1] // HEAD_WIDTH):
        part = values[:, head * HEAD_WIDTH : (head + 1) * HEAD_WIDTH]
        turned.append(part * cosine + pltpu.roll(part, HEAD_WIDTH // 2, 1) * sine)
    return jnp.concatenate(turned, axis=1)


def note_kernel(hidden_ref, lengths_ref, out_ref):
    wide = hidden_ref[...].astype(F32)
    squares = wide * wide
    rows, width = squares.shape
    lanes = squares[:, :LANES]
    for at in range(LANES, width, LANES):
        lanes = lanes + squares[:, at : at + LANES]
    sums = jnp.sum(lanes.T, axis=0, keepdims=True)
    row = lax.broadcasted_iota(jnp.int32, (8, rows), 0)
    out_ref[...] = jnp.where(row == 0, sums, jnp.where(row == 1, lengths_ref[...], 0.0))


def note(hidden, placed_lengths):
    return pl.pallas_call(
        note_kernel,
        out_shape=jax.ShapeDtypeStruct((8, hidden.shape[0]), F32),
        compiler_params=params(),
        cost_estimate=pl.CostEstimate(flops=100000, bytes_accessed=300000, transcendentals=0),
        name="square_sums",
    )(hidden, placed_lengths)


def prep_kernel(
    rank, scalar_ref, here_ref, there_ref, hidden_ref, gain_ref, ids_ref, own_ref, other_ref, weight_hbm,
    inverse_ref, keep_ref, give_ref, shrink_ref, kv_ref, weight_ref, sems,
):
    rows, width = hidden_ref.shape
    model_width = gain_ref.shape[0] * width
    chunks = sems.shape[0]
    depth = width // chunks
    copies = [
        pltpu.make_async_copy(
            weight_hbm.at[pl.ds(c * depth, depth)], weight_ref.at[pl.ds(c * depth, depth)], sems.at[c]
        )
        for c in range(chunks)
    ]
    for copy in copies:
        copy.start()
    total = here_ref[:1] + there_ref[:1]
    inverse_row = lax.rsqrt(total / model_width + EPS)
    inverse = jnp.broadcast_to(inverse_row, (LANES, rows)).T
    inverse_ref[...] = inverse
    gain = gain_ref[pl.ds(scalar_ref[0, 2], 1)].reshape(1, width)
    normed = (hidden_ref[...].astype(F32) * inverse[:, :1] * gain).astype(BF16)
    shrink = jnp.zeros((rows, 3 * rank), F32)
    for side, panel_ref in enumerate((own_ref, other_ref)):
        for j in range(panel_ref.shape[0]):
            part = lax.dot_general(normed, panel_ref[j], (((1,), (1,)), ((), ())), preferred_element_type=F32)
            shrink = shrink + jnp.where(ids_ref[:, :1] == scalar_ref[0, side] + j, part, 0.0)
    half = rows // 2
    packed = jnp.concatenate([shrink[:half, :rank], shrink[half:, :rank]], axis=1)
    tensor, page, _ = shrink_ref.shape
    own_rows = page - half
    for peer in range(tensor):
        shrink_ref[peer, :half] = packed
        shrink_ref[peer, half:] = shrink[peer * own_rows : (peer + 1) * own_rows, rank:]
    total = None
    for c, copy in enumerate(copies):
        copy.wait()
        part = dot(normed[:, c * depth : (c + 1) * depth], weight_ref[c * depth : (c + 1) * depth])
        total = part if total is None else total + part
    kv_ref[...] = total
    parity = scalar_ref[0, 2] % 2
    for pair in range(tensor // 2):
        keep_ref[pair] = kv_ref[pl.ds(pl.multiple_of((2 * pair + parity) * own_rows, own_rows), own_rows)]
        give_ref[pair] = kv_ref[pl.ds(pl.multiple_of((2 * pair + 1 - parity) * own_rows, own_rows), own_rows)]


def prep(scalars, here, there, hidden, gains, ids, weight, own, other, rank, tensor):
    rows, width = hidden.shape
    columns = weight.shape[1]
    chunks = 4 if width % 1024 == 0 else 1
    page = rows // 2 + rows // tensor
    vmem = pl.BlockSpec(memory_space=pltpu.VMEM)
    return pl.pallas_call(
        functools.partial(prep_kernel, rank),
        in_specs=[pl.BlockSpec(memory_space=pltpu.SMEM)] + [vmem] * 7 + [pl.BlockSpec(memory_space=pl.ANY)],
        out_specs=[vmem] * 4,
        out_shape=[
            jax.ShapeDtypeStruct((rows, LANES), F32),
            jax.ShapeDtypeStruct((tensor // 2, rows // tensor, columns), F32),
            jax.ShapeDtypeStruct((tensor // 2, rows // tensor, columns), F32),
            jax.ShapeDtypeStruct((tensor, page, LANES), F32),
        ],
        scratch_shapes=[
            pltpu.VMEM((rows, columns), F32),
            pltpu.VMEM(weight.shape, BF16),
            pltpu.SemaphoreType.DMA((chunks,)),
        ],
        compiler_params=params(),
        cost_estimate=pl.CostEstimate(flops=700000000, bytes_accessed=6000000, transcendentals=0),
        name="norm_key_value_shrink",
    )(scalars, here, there, hidden, gains, ids, own, other, weight)


def query_kernel(count, columns_at, first, scalar_ref, *refs):
    blocks = refs[:count]
    gain_ref, inverse_ref = refs[count : count + 2]
    weight_hbm = refs[-4]
    out_ref, weight_ref, sems = refs[-3:]
    width = blocks[0].shape[1]
    owners = [scalar_ref[0, columns_at + i] for i in range(count)]
    copies = [
        pltpu.make_async_copy(weight_hbm.at[pl.ds(owners[i] * width, width)], weight_ref.at[i], sems.at[i])
        for i in range(count)
    ]
    for copy in copies:
        copy.start()
    inverse = inverse_ref[:, :1]
    total = None if first else refs[count + 2][...]
    for i in range(count):
        gain = gain_ref[pl.ds(owners[i], 1)].reshape(1, width)
        normed = (blocks[i][...].astype(F32) * inverse * gain).astype(BF16)
        copies[i].wait()
        part = dot(normed, weight_ref[i])
        total = part if total is None else total + part
    out_ref[...] = total


def query_step(scalars, columns_at, blocks, gains, weight, inverse, acc):
    rows, width = blocks[0].shape
    columns = weight.shape[1]
    count = len(blocks)
    vmem = pl.BlockSpec(memory_space=pltpu.VMEM)
    operands = list(blocks) + [gains, inverse] + ([] if acc is None else [acc])
    return pl.pallas_call(
        functools.partial(query_kernel, count, columns_at, acc is None),
        in_specs=[pl.BlockSpec(memory_space=pltpu.SMEM)]
        + [vmem] * len(operands)
        + [pl.BlockSpec(memory_space=pl.ANY)],
        out_specs=vmem,
        out_shape=jax.ShapeDtypeStruct((rows, columns), F32),
        scratch_shapes=[pltpu.VMEM((count, width, columns), BF16), pltpu.SemaphoreType.DMA((count,))],
        compiler_params=params(),
        cost_estimate=pl.CostEstimate(flops=500000000, bytes_accessed=5000000, transcendentals=0),
        name="query_products",
    )(scalars, *operands, weight)


def delta_kernel(
    rank, first_ref, parts_ref, ids_ref, own_ids_ref, up_own_ref, up_other_ref, kv_own_ref, kv_other_ref,
    delta_ref, kv_delta_ref,
):
    rows = ids_ref.shape[0]
    half = rows // 2
    kv_width = kv_delta_ref.shape[1] // 2
    total = parts_ref[0]
    for peer in range(1, parts_ref.shape[0]):
        total = total + parts_ref[peer]
    shrink = jnp.concatenate([total[:half, :rank], total[:half, rank:]], axis=0)
    own = total[half:]
    delta = None
    key_delta = value_delta = None
    for side, (up_ref, kv_ref) in enumerate(((up_own_ref, kv_own_ref), (up_other_ref, kv_other_ref))):
        for j in range(up_ref.shape[0]):
            mine = ids_ref[:, :1] == first_ref[0, side] + j
            part = dot(jnp.where(mine, shrink, 0.0).astype(BF16), up_ref[j])
            delta = part if delta is None else delta + part
            kept = jnp.where(own_ids_ref[:, :1] == first_ref[0, side] + j, own, 0.0).astype(BF16)
            key_part = dot(kept[:, :rank], kv_ref[j, 0])
            value_part = dot(kept[:, rank:], kv_ref[j, 1])
            key_delta = key_part if key_delta is None else key_delta + key_part
            value_delta = value_part if value_delta is None else value_delta + value_part
    delta_ref[...] = delta
    kv_delta_ref[:, :kv_width] = key_delta
    kv_delta_ref[:, kv_width:] = value_delta


def deltas(scalars, parts, ids, own_ids, ups, kv_ups, rank):
    rows, own_rows = ids.shape[0], own_ids.shape[0]
    columns = ups[0].shape[2]
    kv_columns = 2 * kv_ups[0].shape[3]
    vmem = pl.BlockSpec(memory_space=pltpu.VMEM)
    return pl.pallas_call(
        functools.partial(delta_kernel, rank),
        in_specs=[pl.BlockSpec(memory_space=pltpu.SMEM)] + [vmem] * 7,
        out_specs=[vmem, vmem],
        out_shape=[
            jax.ShapeDtypeStruct((rows, columns), F32),
            jax.ShapeDtypeStruct((own_rows, kv_columns), F32),
        ],
        compiler_params=params(),
        cost_estimate=pl.CostEstimate(flops=100000000, bytes_accessed=2000000, transcendentals=0),
        name="adapter_terms",
    )(scalars, parts, ids, own_ids, *ups, *kv_ups)


def finish_kernel(
    column_at, scalar_ref, top_ref, bottom_ref, gain_ref, inverse_ref, acc_ref, delta_ref, cosine_ref, sine_ref,
    weight_hbm, out_ref, weight_ref, sems,
):
    width = top_ref.shape[1]
    chunks = sems.shape[0]
    depth = width // chunks
    owner = scalar_ref[0, column_at]
    copies = [
        pltpu.make_async_copy(
            weight_hbm.at[pl.ds(owner * width + c * depth, depth)], weight_ref.at[pl.ds(c * depth, depth)], sems.at[c]
        )
        for c in range(chunks)
    ]
    for copy in copies:
        copy.start()
    gain = gain_ref[pl.ds(owner, 1)].reshape(1, width)
    block = jnp.concatenate([top_ref[...], bottom_ref[...]], axis=0).astype(F32)
    normed = (block * inverse_ref[:, :1] * gain).astype(BF16)
    total = acc_ref[...] + delta_ref[...]
    for c, copy in enumerate(copies):
        copy.wait()
        total = total + dot(normed[:, c * depth : (c + 1) * depth], weight_ref[c * depth : (c + 1) * depth])
    raw = total.astype(BF16).astype(F32)
    out_ref[...] = rotate_heads(raw, cosine_ref[...], sine_ref[...]).astype(BF16)


def finish(scalars, column_at, top, bottom, gains, weight, inverse, acc, delta, cosine, sine):
    width = top.shape[1]
    rows, columns = acc.shape
    chunks = 2 if width % 1024 == 0 else 1
    vmem = pl.BlockSpec(memory_space=pltpu.VMEM)
    return pl.pallas_call(
        functools.partial(finish_kernel, column_at),
        in_specs=[pl.BlockSpec(memory_space=pltpu.SMEM)] + [vmem] * 8 + [pl.BlockSpec(memory_space=pl.ANY)],
        out_specs=vmem,
        out_shape=jax.ShapeDtypeStruct((rows, columns), BF16),
        scratch_shapes=[pltpu.VMEM((width, columns), BF16), pltpu.SemaphoreType.DMA((chunks,))],
        compiler_params=params(),
        cost_estimate=pl.CostEstimate(flops=270000000, bytes_accessed=3000000, transcendentals=0),
        name="query_finish",
    )(scalars, top, bottom, gains, inverse, acc, delta, cosine, sine, weight)


def pair_kernel(scalar_ref, keep_ref, got_ref, *out_refs):
    index = lax.div(scalar_ref[0, 2], 2)
    for distance, out_ref in enumerate(out_refs):
        other = index ^ distance
        out_ref[...] = keep_ref[other] + got_ref[other]


def pair_sums(scalars, keep, got):
    count, own_rows, columns = keep.shape
    vmem = pl.BlockSpec(memory_space=pltpu.VMEM)
    return pl.pallas_call(
        pair_kernel,
        in_specs=[pl.BlockSpec(memory_space=pltpu.SMEM), vmem, vmem],
        out_specs=[vmem] * count,
        out_shape=[jax.ShapeDtypeStruct((own_rows, columns), F32)] * count,
        compiler_params=params(),
        cost_estimate=pl.CostEstimate(flops=100000, bytes_accessed=1500000, transcendentals=0),
        name="pair_sums",
    )(scalars, keep, got)


def fresh_kernel(count, *refs):
    parts = refs[:count]
    delta_ref, cosine_ref, sine_ref, out_ref = refs[count:]
    total = parts[0][...]
    for part in parts[1:]:
        total = total + part[...]
    total = total + delta_ref[...]
    kv_width = total.shape[1] // 2
    out_ref[:, :kv_width] = rotate_heads(total[:, :kv_width], cosine_ref[...], sine_ref[...]).astype(BF16)
    out_ref[:, kv_width:] = total[:, kv_width:].astype(BF16)


def fresh(parts, delta, cosine, sine):
    return pl.pallas_call(
        functools.partial(fresh_kernel, len(parts)),
        out_shape=jax.ShapeDtypeStruct(delta.shape, BF16),
        compiler_params=params(),
        cost_estimate=pl.CostEstimate(flops=100000, bytes_accessed=1000000, transcendentals=0),
        name="new_key_value",
    )(*parts, delta, cosine, sine)


def attend(query_rows, new_key, new_value, cache, lengths):
    tensor, own_rows, columns = query_rows.shape
    positions = cache.shape[2]
    kv_width = cache.shape[3]
    key_heads = kv_width // HEAD_WIDTH
    groups = columns * tensor // kv_width
    scale = 1.0 / math.sqrt(HEAD_WIDTH)
    query_heads = (
        query_rows.reshape(tensor, own_rows, -1, HEAD_WIDTH)
        .transpose(1, 0, 2, 3)
        .reshape(own_rows, key_heads, groups, HEAD_WIDTH)
    )
    keys = cache[:, 0].reshape(own_rows, positions, key_heads, HEAD_WIDTH)
    values = cache[:, 1].reshape(own_rows, positions, key_heads, HEAD_WIDTH)
    fresh_key = new_key.reshape(own_rows, key_heads, HEAD_WIDTH)
    fresh_value = new_value.reshape(own_rows, key_heads, HEAD_WIDTH)
    scores = jnp.einsum("rkgd,rpkd->rkgp", query_heads, keys, preferred_element_type=F32) * scale
    visible = jnp.arange(positions)[None, :] < lengths[:, None]
    scores = jnp.where(visible[:, None, None, :], scores, F32(-1e30))
    new_score = jnp.einsum("rkgd,rkd->rkg", query_heads, fresh_key, preferred_element_type=F32) * scale
    top = jnp.maximum(jnp.max(scores, axis=-1), new_score)
    weights = jnp.exp(scores - top[..., None])
    new_weight = jnp.exp(new_score - top)
    denominator = jnp.sum(weights, axis=-1) + new_weight
    cache_weights = (weights / denominator[..., None]).astype(BF16)
    fresh_weights = (new_weight / denominator).astype(BF16)
    mixed = jnp.einsum("rkgp,rpkd->rkgd", cache_weights, values, preferred_element_type=F32)
    mixed = mixed + fresh_weights.astype(F32)[..., None] * fresh_value.astype(F32)[:, :, None, :]
    return mixed.reshape(own_rows, -1).astype(BF16)


def make_body(mesh):
    tensor = mesh.shape["tensor"]
    shards = mesh.shape["adapter"]
    order = ring_order(tensor)
    place_of = [order.index(t) for t in range(tensor)]
    right = [(order[i], order[(i + 1) % tensor]) for i in range(tensor)]
    left = [(b, a) for a, b in right]
    swap = [(i, shards - 1 - i) for i in range(shards)]

    distances = [1 << k for k in range(tensor.bit_length() - 1)]

    def table(own_adapters):
        lines = []
        for side in range(shards):
            for position in range(tensor):
                place = place_of[position]
                steps = [0] + [sign * step for step in range(1, tensor // 2) for sign in (-1, 1)] + [tensor // 2]
                owners = [order[(place + step) % tensor] for step in steps]
                lines.append([side * own_adapters, (shards - 1 - side) * own_adapters, position] + owners)
        return np.array(lines, np.int32)

    def everyone(x):
        return lax.all_to_all(x, "tensor", 0, 0, tiled=True)

    def body(
        hidden,
        input_norm_scale,
        query_weight,
        key_value_weight,
        adapter_down_weight,
        adapter_up_query,
        adapter_up_key_value,
        request_adapter,
        key_value_cache,
        lengths,
    ):
        position = lax.axis_index("tensor")
        side = lax.axis_index("adapter")
        local = hidden[0]
        rows, width = local.shape
        own_rows = rows // tensor
        start = position * own_rows
        own_adapters = adapter_down_weight.shape[0]
        rank = adapter_up_query.shape[1]
        kv_width = adapter_up_key_value.shape[3]
        gains = input_norm_scale.reshape(tensor, 1, width)
        ids = jnp.broadcast_to(request_adapter[0][:, None], (rows, LANES))
        own_ids = lax.dynamic_slice_in_dim(ids, start, own_rows, 0)
        scalars = lax.dynamic_slice_in_dim(jnp.asarray(table(own_adapters)), side * tensor + position, 1, 0)

        placed = lax.dynamic_update_slice_in_dim(jnp.zeros((rows,), F32), lengths[0].astype(F32), start, 0)
        here = note(local, placed[None])
        sent = after(local, here)
        from_left = lax.ppermute(sent, "tensor", right)
        from_right = lax.ppermute(sent, "tensor", left)
        for distance in distances:
            there = lax.ppermute(here, "tensor", [(t, t ^ distance) for t in range(tensor)])
            if distance != distances[-1]:
                here = here + there
        cosine, sine = rotary_tables(here[1] + there[1])
        own_cosine = lax.dynamic_slice_in_dim(cosine, start, own_rows, 0)
        own_sine = lax.dynamic_slice_in_dim(sine, start, own_rows, 0)

        own_down = adapter_down_weight.transpose(0, 2, 1)
        other_down, other_up, other_kv = (
            lax.ppermute(w, "adapter", swap) for w in (own_down, adapter_up_query, adapter_up_key_value)
        )
        inverse, keep, give, shrink = prep(
            scalars, here, there, local, gains, ids, key_value_weight, own_down, other_down, rank, tensor
        )
        shrink_parts = everyone(shrink)
        got = lax.ppermute(give, "tensor", [(t, t ^ 1) for t in range(tensor)])
        sums = pair_sums(scalars, keep, got)
        kv_parts = [sums[0]] + [
            lax.ppermute(sums[d], "tensor", [(t, t ^ (2 * d)) for t in range(tensor)]) for d in range(1, tensor // 2)
        ]
        delta, kv_delta = deltas(
            scalars, shrink_parts, ids, own_ids, (adapter_up_query, other_up), (adapter_up_key_value, other_kv), rank
        )

        early = tensor // 2 - 1
        arrived = [local, from_left, from_right]
        acc = None
        column_at = 3
        half = rows // 2
        for step in range(2, tensor // 2 + 1):
            if step == early:
                from_left, from_right = after((from_left, from_right), inverse)
            if step == tensor // 2:
                acc = query_step(scalars, column_at, arrived, gains, query_weight, inverse, acc)
                column_at += len(arrived)
                arrived = []
                last_left, last_right = after((from_left[:half], from_right[half:]), acc)
                top = lax.ppermute(last_left, "tensor", right)
                bottom = lax.ppermute(last_right, "tensor", left)
            else:
                from_left = lax.ppermute(from_left, "tensor", right)
                from_right = lax.ppermute(from_right, "tensor", left)
                if step == early:
                    acc = query_step(scalars, column_at, arrived, gains, query_weight, inverse, acc)
                    column_at += len(arrived)
                    arrived = []
                arrived += [from_left, from_right]
        query = finish(
            scalars, 2 + tensor, top, bottom, gains, query_weight, inverse, acc, delta, cosine, sine
        )
        query_rows = everyone(query.reshape(tensor, own_rows, -1))

        newest = fresh(kv_parts, kv_delta, own_cosine, own_sine)
        attended = attend(query_rows, newest[:, :kv_width], newest[:, kv_width:], key_value_cache[0], lengths[0])
        return attended[None], newest.reshape(1, own_rows, 2, kv_width)

    return body


def solution(mesh):
    return jax.shard_map(
        make_body(mesh),
        mesh=mesh,
        in_specs=(
            P("adapter", "group", "tensor"),
            P(),
            P(None, "tensor"),
            P("tensor", None),
            P(("group", "adapter"), "tensor", None),
            P(("group", "adapter"), None, "tensor"),
            P(("group", "adapter"), None, None, None),
            P("adapter", "group"),
            P("adapter", ("group", "tensor"), None, None, None),
            P("adapter", ("group", "tensor")),
        ),
        out_specs=(
            P("adapter", ("group", "tensor"), None),
            P("adapter", ("group", "tensor"), None, None),
        ),
        check_vma=False,
    )
```

```python
import functools
import math

import jax
import jax.numpy as jnp
import numpy as np
from jax import lax
from jax.experimental import pallas as pl
from jax.experimental.pallas import tpu as pltpu
from jax.sharding import PartitionSpec as P

HEAD_WIDTH = 128
LANES = 128
EPS = 1e-05
THETA = 500000.0
UNROLL = 4
NARROW = jnp.float16
SLOTS = 4
F32 = jnp.float32
BF16 = jnp.bfloat16


def ring_order(size):
    if size == 8:
        return [0, 2, 4, 6, 7, 5, 3, 1]
    return list(range(size))


def dot(a, b):
    return jnp.dot(a, b, preferred_element_type=F32)


def params(mib=16):
    return pltpu.CompilerParams(vmem_limit_bytes=mib * 1024 * 1024)


def after(value, *others):
    return lax.optimization_barrier((value, *others))[0]


VMEM = pl.BlockSpec(memory_space=pltpu.VMEM)
SMEM = pl.BlockSpec(memory_space=pltpu.SMEM)
HBM = pl.BlockSpec(memory_space=pltpu.HBM)


def in_hbm(value):
    return pltpu.with_memory_space_constraint(value, pltpu.HBM)


def rotary_tables(positions):
    half = HEAD_WIDTH // 2
    frequency = THETA ** (-(jnp.arange(half).astype(F32) * 2.0 / HEAD_WIDTH))
    angles = positions.astype(F32)[:, None] * frequency[None, :]
    cosine = jnp.cos(angles)
    sine = jnp.sin(angles)
    return jnp.concatenate([cosine, cosine], axis=1), jnp.concatenate([-sine, sine], axis=1)


def rotate_heads(values, cosine, sine):
    turned = []
    for head in range(values.shape[1] // HEAD_WIDTH):
        part = values[:, head * HEAD_WIDTH : (head + 1) * HEAD_WIDTH]
        turned.append(part * cosine + pltpu.roll(part, HEAD_WIDTH // 2, 1) * sine)
    return jnp.concatenate(turned, axis=1)


def pack_rows(values):
    most = jnp.max(jnp.abs(values), axis=1, keepdims=True)
    exponent = jnp.ceil(jnp.log2(jnp.maximum(most, 1e-30)))
    scaled = values * jnp.exp2(14.0 - exponent)
    return jnp.concatenate([scaled, jnp.broadcast_to(exponent, (values.shape[0], LANES))], axis=1)


def unpack_rows(values):
    width = values.shape[1] - LANES
    return values[:, :width] * jnp.exp2(values[:, width : width + 1] - 14.0)


def lane_sums(block):
    wide = block.astype(F32)
    squares = wide * wide
    lanes = squares[:, :LANES]
    for at in range(LANES, squares.shape[1], LANES):
        lanes = lanes + squares[:, at : at + LANES]
    return lanes


def sums_kernel(first, *refs):
    out_ref = refs[-1]
    half = out_ref.shape[0] // 2
    tops = refs[0:-1:2] if first else refs[0:-2:2]
    bottoms = refs[1:-1:2] if first else refs[1:-2:2]
    top = None if first else refs[-2][:half]
    bottom = None if first else refs[-2][half:]
    for top_ref, bottom_ref in zip(tops, bottoms):
        more, below = lane_sums(top_ref[...]), lane_sums(bottom_ref[...])
        top = more if top is None else top + more
        bottom = below if bottom is None else bottom + below
    out_ref[:half] = top
    out_ref[half:] = bottom


def square_sums(blocks, before):
    flat = [half for block in blocks for half in block]
    rows = 2 * flat[0].shape[0]
    operands = flat + ([] if before is None else [before])
    return pl.pallas_call(
        functools.partial(sums_kernel, before is None),
        in_specs=[VMEM] * len(operands),
        out_specs=VMEM,
        out_shape=jax.ShapeDtypeStruct((rows, LANES), F32),
        compiler_params=params(),
        cost_estimate=pl.CostEstimate(flops=1000000, bytes_accessed=600000, transcendentals=0),
        name="square_sums",
    )(*operands)


def id_column(request_ref):
    rows = request_ref.shape[1]
    return jnp.broadcast_to(request_ref[...].astype(F32), (LANES, rows)).T.astype(jnp.int32)


def prep_kernel(
    rank, scalar_ref, sums_ref, last_top_ref, last_bottom_ref, top_ref, bottom_ref, request_ref, other_ref,
    gain_hbm, own_hbm, weight_hbm, inverse_ref, keep_ref, give_ref, shrink_ref,
    kv_ref, gain_ref, own_ref, weight_ref, sems,
):
    rows, width = inverse_ref.shape[0], top_ref.shape[1]
    model_width = gain_hbm.shape[0] * width
    chunks = sems.shape[0] - 2
    depth = width // chunks
    first = [
        pltpu.make_async_copy(gain_hbm.at[scalar_ref[0, 2]], gain_ref, sems.at[chunks]),
        pltpu.make_async_copy(own_hbm, own_ref, sems.at[chunks + 1]),
    ]
    copies = [
        pltpu.make_async_copy(
            weight_hbm.at[pl.ds(c * depth, depth)], weight_ref.at[pl.ds(c * depth, depth)], sems.at[c]
        )
        for c in range(chunks)
    ]
    for copy in first + copies:
        copy.start()
    last = jnp.concatenate([lane_sums(last_top_ref[...]), lane_sums(last_bottom_ref[...])], axis=0)
    total = jnp.sum((sums_ref[...] + last).T, axis=0, keepdims=True)
    inverse_row = lax.rsqrt(total / model_width + EPS)
    inverse = jnp.broadcast_to(inverse_row, (LANES, rows)).T
    inverse_ref[...] = inverse
    ids = id_column(request_ref)
    first[0].wait()
    block = jnp.concatenate([top_ref[...], bottom_ref[...]], axis=0).astype(F32)
    normed = (block * inverse[:, :1] * gain_ref[...]).astype(BF16)
    first[1].wait()
    shrink = jnp.zeros((rows, 3 * rank), F32)
    for side, panel_ref in enumerate((own_ref, other_ref)):
        for j in range(panel_ref.shape[0]):
            part = lax.dot_general(normed, panel_ref[j], (((1,), (1,)), ((), ())), preferred_element_type=F32)
            shrink = shrink + jnp.where(ids[:, :1] == scalar_ref[0, side] + j, part, 0.0)
    half = rows // 2
    packed = jnp.concatenate([shrink[:half, :rank], shrink[half:, :rank]], axis=1)
    tensor, page, _ = shrink_ref.shape
    own_rows = page - half
    for peer in range(tensor):
        shrink_ref[peer, :half] = packed
        shrink_ref[peer, half:] = shrink[peer * own_rows : (peer + 1) * own_rows, rank:]
    total = None
    for c, copy in enumerate(copies):
        copy.wait()
        part = dot(normed[:, c * depth : (c + 1) * depth], weight_ref[c * depth : (c + 1) * depth])
        total = part if total is None else total + part
    kv_ref[...] = total
    parity = scalar_ref[0, 2] % 2
    for pair in range(tensor // 2):
        keep_ref[pair] = kv_ref[pl.ds(pl.multiple_of((2 * pair + parity) * own_rows, own_rows), own_rows)]
        give_ref[pair] = pack_rows(
            kv_ref[pl.ds(pl.multiple_of((2 * pair + 1 - parity) * own_rows, own_rows), own_rows)]
        )


def prep(scalars, sums, last, local, request, gains, weight, own, other, rank, tensor):
    half, width = local[0].shape
    rows = 2 * half
    columns = weight.shape[1]
    chunks = 4 if width % 1024 == 0 else 1
    page = rows // 2 + rows // tensor
    return pl.pallas_call(
        functools.partial(prep_kernel, rank),
        in_specs=[SMEM] + [VMEM] * 7 + [HBM] * 3,
        out_specs=[VMEM] * 4,
        out_shape=[
            jax.ShapeDtypeStruct((rows, LANES), F32),
            pltpu.HBM((tensor // 2, rows // tensor, columns), F32),
            jax.ShapeDtypeStruct((tensor // 2, rows // tensor, columns + LANES), F32),
            pltpu.HBM((tensor, page, LANES), F32),
        ],
        scratch_shapes=[
            pltpu.VMEM((rows, columns), F32),
            pltpu.VMEM((1, width), F32),
            pltpu.VMEM(own.shape, BF16),
            pltpu.VMEM(weight.shape, BF16),
            pltpu.SemaphoreType.DMA((chunks + 2,)),
        ],
        compiler_params=params(),
        cost_estimate=pl.CostEstimate(flops=700000000, bytes_accessed=6000000, transcendentals=0),
        name="norm_key_value_shrink",
    )(scalars, sums, *last, *local, in_hbm(request), other, in_hbm(gains), in_hbm(own), in_hbm(weight))


def query_kernel(count, columns_at, scalar_ref, *refs):
    blocks = refs[: 2 * count]
    inverse_ref, gain_hbm, weight_hbm, out_ref, gain_ref, weight_ref, sems = refs[2 * count :]
    width = blocks[0].shape[1]
    slots = weight_ref.shape[0]
    owners = [scalar_ref[0, columns_at + i] for i in range(count)]
    gain_copy = pltpu.make_async_copy(gain_hbm, gain_ref, sems.at[slots])

    def fetch(i):
        return pltpu.make_async_copy(
            weight_hbm.at[pl.ds(pl.multiple_of(owners[i] * width, width), width)],
            weight_ref.at[i % slots],
            sems.at[i % slots],
        )

    gain_copy.start()
    for i in range(min(slots, count)):
        fetch(i).start()
    gain_copy.wait()
    inverse = inverse_ref[:, :1]
    for i in range(count):
        gain = gain_ref[pl.ds(owners[i], 1)].reshape(1, width)
        block = jnp.concatenate([blocks[2 * i][...], blocks[2 * i + 1][...]], axis=0).astype(F32)
        normed = (block * inverse * gain).astype(BF16)
        fetch(i).wait()
        part = dot(normed, weight_ref[i % slots])
        out_ref[...] = part if i == 0 else out_ref[...] + part
        if i + slots < count:
            fetch(i + slots).start()


def query_products(scalars, columns_at, blocks, gains, weight, inverse):
    width = blocks[0][0].shape[1]
    columns = weight.shape[1]
    count = len(blocks)
    flat = [half for block in blocks for half in block]
    slots = min(SLOTS, count)
    return pl.pallas_call(
        functools.partial(query_kernel, count, columns_at),
        in_specs=[SMEM] + [VMEM] * (2 * count + 1) + [HBM] * 2,
        out_specs=VMEM,
        out_shape=jax.ShapeDtypeStruct((inverse.shape[0], columns), F32),
        scratch_shapes=[
            pltpu.VMEM(gains.shape, F32),
            pltpu.VMEM((slots, width, columns), BF16),
            pltpu.SemaphoreType.DMA((slots + 1,)),
        ],
        compiler_params=params(16),
        cost_estimate=pl.CostEstimate(flops=2000000000, bytes_accessed=17000000, transcendentals=0),
        name="query_products",
    )(scalars, *flat, inverse, in_hbm(gains), in_hbm(weight))


def finish_kernel(
    rank, first_ref, parts_ref, request_ref, acc_ref, up_own_hbm, up_other_hbm, kv_own_hbm, kv_other_hbm,
    out_ref, kv_delta_ref, up_own_ref, up_other_ref, kv_own_ref, kv_other_ref, column_ref, sems,
):
    rows = request_ref.shape[1]
    half = rows // 2
    kv_width = kv_delta_ref.shape[1] // 2
    sources = (up_own_hbm, up_other_hbm, kv_own_hbm, kv_other_hbm)
    targets = (up_own_ref, up_other_ref, kv_own_ref, kv_other_ref)
    copies = [pltpu.make_async_copy(sources[i], targets[i], sems.at[i]) for i in range(4)]
    for copy in copies:
        copy.start()
    ids_ref = id_column(request_ref)
    total = parts_ref[0]
    for peer in range(1, parts_ref.shape[0]):
        total = total + parts_ref[peer]
    for copy in copies:
        copy.wait()
    shrink = jnp.concatenate([total[:half, :rank], total[:half, rank:]], axis=0)
    own_rows = kv_delta_ref.shape[0]
    own = total[half:]
    column_ref[...] = ids_ref
    own_ids = column_ref[pl.ds(pl.multiple_of(first_ref[0, 2] * own_rows, own_rows), own_rows)]
    delta = None
    key_delta = value_delta = None
    for side, (up_ref, kv_ref) in enumerate(((up_own_ref, kv_own_ref), (up_other_ref, kv_other_ref))):
        for j in range(up_ref.shape[0]):
            mine = ids_ref[:, :1] == first_ref[0, side] + j
            part = dot(jnp.where(mine, shrink, 0.0).astype(BF16), up_ref[j])
            delta = part if delta is None else delta + part
            kept = jnp.where(own_ids[:, :1] == first_ref[0, side] + j, own, 0.0).astype(BF16)
            key_part = dot(kept[:, :rank], kv_ref[j, 0])
            value_part = dot(kept[:, rank:], kv_ref[j, 1])
            key_delta = key_part if key_delta is None else key_delta + key_part
            value_delta = value_part if value_delta is None else value_delta + value_part
    out_ref[...] = (acc_ref[...] + delta).astype(BF16)
    kv_delta_ref[:, :kv_width] = key_delta
    kv_delta_ref[:, kv_width:] = value_delta


def finish(scalars, parts, request, ups, kv_ups, acc, rank):
    rows = request.shape[1]
    own_rows = rows // parts.shape[0]
    columns = ups[0].shape[2]
    kv_columns = 2 * kv_ups[0].shape[3]
    return pl.pallas_call(
        functools.partial(finish_kernel, rank),
        in_specs=[SMEM] + [VMEM] * 3 + [HBM] * 4,
        out_specs=[VMEM, VMEM],
        out_shape=[
            jax.ShapeDtypeStruct((rows, columns), BF16),
            jax.ShapeDtypeStruct((own_rows, kv_columns), F32),
        ],
        scratch_shapes=[
            pltpu.VMEM(ups[0].shape, BF16),
            pltpu.VMEM(ups[1].shape, BF16),
            pltpu.VMEM(kv_ups[0].shape, BF16),
            pltpu.VMEM(kv_ups[1].shape, BF16),
            pltpu.VMEM((rows, LANES), jnp.int32),
            pltpu.SemaphoreType.DMA((4,)),
        ],
        compiler_params=params(),
        cost_estimate=pl.CostEstimate(flops=100000000, bytes_accessed=2000000, transcendentals=0),
        name="adapter_terms",
    )(scalars, parts, in_hbm(request), acc, *[in_hbm(value) for value in (*ups, *kv_ups)])


def pair_kernel(scalar_ref, keep_ref, got_ref, *out_refs):
    index = lax.div(scalar_ref[0, 2], 2)
    for distance, out_ref in enumerate(out_refs):
        other = index ^ distance
        total = keep_ref[other] + unpack_rows(got_ref[other])
        out_ref[...] = total if distance == 0 else pack_rows(total)


def pair_sums(scalars, keep, got):
    count, own_rows, columns = keep.shape
    return pl.pallas_call(
        pair_kernel,
        in_specs=[SMEM, VMEM, VMEM],
        out_specs=[VMEM] * count,
        out_shape=[jax.ShapeDtypeStruct((own_rows, columns), F32)]
        + [jax.ShapeDtypeStruct((own_rows, columns + LANES), F32)] * (count - 1),
        compiler_params=params(),
        cost_estimate=pl.CostEstimate(flops=100000, bytes_accessed=1500000, transcendentals=0),
        name="pair_sums",
    )(scalars, in_hbm(keep), got)


def fresh_kernel(count, *refs):
    parts = refs[:count]
    delta_ref, cosine_ref, sine_ref, out_ref, heads_ref = refs[count:]
    total = parts[0][...]
    for part in parts[1:]:
        total = total + unpack_rows(part[...])
    total = total + delta_ref[...]
    kv_width = total.shape[1] // 2
    newest = jnp.concatenate(
        [rotate_heads(total[:, :kv_width], cosine_ref[...], sine_ref[...]), total[:, kv_width:]], axis=1
    ).astype(BF16)
    out_ref[:, 0, :] = newest[:, :kv_width]
    out_ref[:, 1, :] = newest[:, kv_width:]
    spread = newest.astype(F32)
    for head in range(heads_ref.shape[1]):
        heads_ref[:, head, :] = spread[:, head * HEAD_WIDTH : (head + 1) * HEAD_WIDTH]


def fresh(parts, delta, cosine, sine):
    own_rows, columns = delta.shape
    return pl.pallas_call(
        functools.partial(fresh_kernel, len(parts)),
        out_shape=[
            jax.ShapeDtypeStruct((own_rows, 2, columns // 2), BF16),
            jax.ShapeDtypeStruct((own_rows, columns // HEAD_WIDTH, HEAD_WIDTH), F32),
        ],
        compiler_params=params(),
        cost_estimate=pl.CostEstimate(flops=100000, bytes_accessed=1000000, transcendentals=0),
        name="new_key_value",
    )(*parts, delta, cosine, sine)


def attend_kernel(
    lengths_ref, query_ref, newest_ref, cosine_ref, sine_ref, cache_hbm, out_ref, query_heads_ref, scores_ref, weights_ref, fresh_ref,
    cache_ref, sems,
):
    tensor, own_rows, columns = query_ref.shape
    per_peer = columns // HEAD_WIDTH
    positions = cache_ref.shape[2]
    key_heads = cache_ref.shape[3] // HEAD_WIDTH
    heads = tensor * per_peer
    groups = heads // key_heads
    scale = 1.0 / math.sqrt(HEAD_WIDTH)
    pair = 2 * groups
    parts = sems.shape[1]
    step = own_rows // parts
    copies = [
        [
            pltpu.make_async_copy(
                cache_hbm.at[pl.ds(i * step, step), which], cache_ref.at[which, pl.ds(i * step, step)], sems.at[which, i]
            )
            for i in range(parts)
        ]
        for which in range(2)
    ]
    for copy in copies[0] + copies[1]:
        copy.start()
    for peer in range(tensor):
        part = rotate_heads(query_ref[peer].astype(F32), cosine_ref[...], sine_ref[...]).astype(BF16).astype(F32)
        for j in range(per_peer):
            query_heads_ref[:, peer * per_peer + j, :] = part[:, j * HEAD_WIDTH : (j + 1) * HEAD_WIDTH]
    side = lax.broadcasted_iota(jnp.int32, (pair, 2 * HEAD_WIDTH), 0) < groups
    on_side = side == (lax.broadcasted_iota(jnp.int32, (pair, 2 * HEAD_WIDTH), 1) < HEAD_WIDTH)
    lane = lax.broadcasted_iota(jnp.int32, (heads, positions), 1)

    def to_heads(part):
        return jnp.broadcast_to(part[:, None, :], (key_heads, groups, HEAD_WIDTH)).reshape(heads, HEAD_WIDTH)

    def score_step(row, carry):
        query = query_heads_ref[row]
        for k in range(0, key_heads, 2):
            two = query[k * groups : (k + 2) * groups]
            spread = jnp.where(on_side, jnp.concatenate([two, two], axis=1), 0.0).astype(BF16)
            keys = cache_ref[0, row, :, k * HEAD_WIDTH : (k + 2) * HEAD_WIDTH]
            scores_ref[row, k * groups : (k + 2) * groups] = lax.dot_general(
                spread, keys, (((1,), (1,)), ((), ())), preferred_element_type=F32
            )
        return carry

    def weight_step(row, carry):
        score = jnp.where(lane < lengths_ref[0, row], scores_ref[row] * scale, -1e30)
        new_key = to_heads(newest_ref[row, :key_heads])
        new_value = to_heads(newest_ref[row, key_heads:])
        new_score = jnp.sum(query_heads_ref[row] * new_key, axis=1, keepdims=True) * scale
        top = jnp.maximum(jnp.max(score, axis=1, keepdims=True), new_score)
        weights = jnp.exp(score - top)
        new_weight = jnp.exp(new_score - top)
        denominator = jnp.sum(weights, axis=1, keepdims=True) + new_weight
        weights_ref[row] = (weights / denominator).astype(BF16)
        fresh_ref[row] = (new_weight / denominator).astype(BF16).astype(F32) * new_value
        return carry

    def value_step(row, carry):
        for k in range(0, key_heads, 2):
            values = cache_ref[1, row, :, k * HEAD_WIDTH : (k + 2) * HEAD_WIDTH]
            both = dot(weights_ref[row, k * groups : (k + 2) * groups], values)
            query_heads_ref[row, k * groups : (k + 1) * groups] = (
                both[:groups, :HEAD_WIDTH] + fresh_ref[row, k * groups : (k + 1) * groups]
            )
            query_heads_ref[row, (k + 1) * groups : (k + 2) * groups] = (
                both[groups:, HEAD_WIDTH:] + fresh_ref[row, (k + 1) * groups : (k + 2) * groups]
            )
        return carry

    for i, copy in enumerate(copies[0]):
        copy.wait()
        lax.fori_loop(i * step, (i + 1) * step, score_step, 0, unroll=True)
    lax.fori_loop(0, own_rows, weight_step, 0, unroll=UNROLL)
    for i, copy in enumerate(copies[1]):
        copy.wait()
        lax.fori_loop(i * step, (i + 1) * step, value_step, 0, unroll=True)
    for head in range(heads):
        out_ref[:, head * HEAD_WIDTH : (head + 1) * HEAD_WIDTH] = query_heads_ref[:, head, :].astype(BF16)


def attend(query_rows, newest_heads, cosine, sine, cache, lengths):
    tensor, own_rows, columns = query_rows.shape
    heads = tensor * columns // HEAD_WIDTH
    return pl.pallas_call(
        attend_kernel,
        in_specs=[SMEM] + [VMEM] * 4 + [HBM],
        out_specs=VMEM,
        out_shape=jax.ShapeDtypeStruct((own_rows, tensor * columns), BF16),
        scratch_shapes=[
            pltpu.VMEM((own_rows, heads, HEAD_WIDTH), F32),
            pltpu.VMEM((own_rows, heads, cache.shape[2]), F32),
            pltpu.VMEM((own_rows, heads, cache.shape[2]), BF16),
            pltpu.VMEM((own_rows, heads, HEAD_WIDTH), F32),
            pltpu.VMEM((2, own_rows) + cache.shape[2:], BF16),
            pltpu.SemaphoreType.DMA((2, 4)),
        ],
        compiler_params=params(),
        cost_estimate=pl.CostEstimate(flops=400000000, bytes_accessed=7000000, transcendentals=100000),
        name="attention",
    )(lengths, query_rows, newest_heads, cosine, sine, in_hbm(cache))


def make_body(mesh):
    tensor = mesh.shape["tensor"]
    shards = mesh.shape["adapter"]
    order = ring_order(tensor)
    place_of = [order.index(t) for t in range(tensor)]
    right = [(order[i], order[(i + 1) % tensor]) for i in range(tensor)]
    left = [(b, a) for a, b in right]
    swap = [(i, shards - 1 - i) for i in range(shards)]

    def table(own_adapters):
        lines = []
        for side in range(shards):
            for position in range(tensor):
                place = place_of[position]
                steps = [0] + [sign * step for step in range(1, tensor // 2) for sign in (-1, 1)] + [tensor // 2]
                owners = [order[(place + step) % tensor] for step in steps]
                lines.append([side * own_adapters, (shards - 1 - side) * own_adapters, position] + owners)
        return np.array(lines, np.int32)

    def everyone(x):
        return lax.all_to_all(x, "tensor", 0, 0, tiled=True)

    def go(x, pairs):
        return lax.ppermute(x, "tensor", pairs)

    def body(
        hidden,
        input_norm_scale,
        query_weight,
        key_value_weight,
        adapter_down_weight,
        adapter_up_query,
        adapter_up_key_value,
        request_adapter,
        key_value_cache,
        lengths,
    ):
        position = lax.axis_index("tensor")
        side = lax.axis_index("adapter")
        rows, width = hidden.shape[1:]
        own_rows = rows // tensor
        half = rows // 2
        own_adapters = adapter_down_weight.shape[0]
        rank = adapter_up_query.shape[1]
        kv_width = adapter_up_key_value.shape[3]
        gains = input_norm_scale.reshape(tensor, 1, width)
        scalars = lax.dynamic_slice_in_dim(jnp.asarray(table(own_adapters)), side * tensor + position, 1, 0)
        own_down = adapter_down_weight.transpose(0, 2, 1)
        other_down, other_up, other_kv = (
            lax.ppermute(w, "adapter", swap) for w in (own_down, adapter_up_query, adapter_up_key_value)
        )
        cosine, sine = rotary_tables(lengths[0])

        local = (hidden[0, :half], hidden[0, half:])
        from_left = from_right = local
        blocks = []
        sums = None
        fresh_blocks = [local]
        for step in range(1, tensor // 2):
            top_left = go(from_left[0], right)
            bottom_right = go(from_right[1], left)
            top_right = go(from_right[0], left)
            bottom_left = go(from_left[1], right)
            from_left, from_right = (top_left, bottom_left), (top_right, bottom_right)
            if step == tensor // 2 - 1:
                sums = square_sums(fresh_blocks, sums)
                fresh_blocks = []
            blocks += [from_left, from_right]
            fresh_blocks += [from_left, from_right]
        last = (go(from_left[0], right), go(from_right[1], left))
        sums = square_sums(fresh_blocks, sums)
        blocks.append(last)

        inverse, keep, give, shrink = prep(
            scalars, sums, last, local, request_adapter, gains, key_value_weight, own_down, other_down, rank, tensor
        )
        shrink_parts = everyone(shrink)
        got = go(give.astype(NARROW), [(t, t ^ 1) for t in range(tensor)])
        pair = pair_sums(scalars, keep, got.astype(F32))
        kv_parts = [pair[0]] + [
            go(pair[d].astype(NARROW), [(t, t ^ (2 * d)) for t in range(tensor)]).astype(F32)
            for d in range(1, tensor // 2)
        ]
        acc = query_products(scalars, 3, [local] + blocks, gains, query_weight, inverse)
        query, kv_delta = finish(
            scalars, shrink_parts, request_adapter, (adapter_up_query, other_up), (adapter_up_key_value, other_kv), after(acc, *pair), rank
        )
        query_rows = everyone(query.reshape(tensor, own_rows, -1))
        newest, newest_heads = fresh(kv_parts, kv_delta, cosine, sine)
        attended = attend(query_rows, newest_heads, cosine, sine, key_value_cache[0], lengths)
        return attended[None], newest[None]

    return body


def solution(mesh):
    return jax.shard_map(
        make_body(mesh),
        mesh=mesh,
        in_specs=(
            P("adapter", "group", "tensor"),
            P(),
            P(None, "tensor"),
            P("tensor", None),
            P(("group", "adapter"), "tensor", None),
            P(("group", "adapter"), None, "tensor"),
            P(("group", "adapter"), None, None, None),
            P("adapter", "group"),
            P("adapter", ("group", "tensor"), None, None, None),
            P("adapter", ("group", "tensor")),
        ),
        out_specs=(
            P("adapter", ("group", "tensor"), None),
            P("adapter", ("group", "tensor"), None, None),
        ),
        check_vma=False,
    )
```

```python
import functools
import math

import jax
import jax.numpy as jnp
import numpy as np
from jax import lax
from jax.experimental import pallas as pl
from jax.experimental.pallas import tpu as pltpu
from jax.sharding import PartitionSpec as P

HEAD_WIDTH = 128
LANES = 128
EPS = 1e-05
THETA = 500000.0
UNROLL = 4
NARROW = jnp.float16
SLOTS = 4
F32 = jnp.float32
BF16 = jnp.bfloat16


def ring_order(size):
    if size == 8:
        return [0, 2, 4, 6, 7, 5, 3, 1]
    return list(range(size))


def dot(a, b):
    return jnp.dot(a, b, preferred_element_type=F32)


def params(mib=16):
    return pltpu.CompilerParams(vmem_limit_bytes=mib * 1024 * 1024)


def after(value, *others):
    return lax.optimization_barrier((value, *others))[0]


VMEM = pl.BlockSpec(memory_space=pltpu.VMEM)
SMEM = pl.BlockSpec(memory_space=pltpu.SMEM)
HBM = pl.BlockSpec(memory_space=pltpu.HBM)


def in_hbm(value):
    return pltpu.with_memory_space_constraint(value, pltpu.HBM)


def rotary_tables(positions):
    half = HEAD_WIDTH // 2
    frequency = THETA ** (-(jnp.arange(half).astype(F32) * 2.0 / HEAD_WIDTH))
    angles = positions.astype(F32)[:, None] * frequency[None, :]
    cosine = jnp.cos(angles)
    sine = jnp.sin(angles)
    return jnp.concatenate([cosine, cosine], axis=1), jnp.concatenate([-sine, sine], axis=1)


def rotate_heads(values, cosine, sine):
    turned = []
    for head in range(values.shape[1] // HEAD_WIDTH):
        part = values[:, head * HEAD_WIDTH : (head + 1) * HEAD_WIDTH]
        turned.append(part * cosine + pltpu.roll(part, HEAD_WIDTH // 2, 1) * sine)
    return jnp.concatenate(turned, axis=1)


def pack_rows(values):
    most = jnp.max(jnp.abs(values), axis=1, keepdims=True)
    exponent = jnp.ceil(jnp.log2(jnp.maximum(most, 1e-30)))
    scaled = values * jnp.exp2(14.0 - exponent)
    return jnp.concatenate([scaled, jnp.broadcast_to(exponent, (values.shape[0], LANES))], axis=1)


def unpack_rows(values):
    width = values.shape[1] - LANES
    return values[:, :width] * jnp.exp2(values[:, width : width + 1] - 14.0)


def lane_sums(block):
    wide = block.astype(F32)
    squares = wide * wide
    lanes = squares[:, :LANES]
    for at in range(LANES, squares.shape[1], LANES):
        lanes = lanes + squares[:, at : at + LANES]
    return lanes


def sums_kernel(first, *refs):
    out_ref = refs[-1]
    half = out_ref.shape[0] // 2
    tops = refs[0:-1:2] if first else refs[0:-2:2]
    bottoms = refs[1:-1:2] if first else refs[1:-2:2]
    top = None if first else refs[-2][:half]
    bottom = None if first else refs[-2][half:]
    for top_ref, bottom_ref in zip(tops, bottoms):
        more, below = lane_sums(top_ref[...]), lane_sums(bottom_ref[...])
        top = more if top is None else top + more
        bottom = below if bottom is None else bottom + below
    out_ref[:half] = top
    out_ref[half:] = bottom


def square_sums(blocks, before):
    flat = [half for block in blocks for half in block]
    rows = 2 * flat[0].shape[0]
    operands = flat + ([] if before is None else [before])
    return pl.pallas_call(
        functools.partial(sums_kernel, before is None),
        in_specs=[VMEM] * len(operands),
        out_specs=VMEM,
        out_shape=jax.ShapeDtypeStruct((rows, LANES), F32),
        compiler_params=params(),
        cost_estimate=pl.CostEstimate(flops=1000000, bytes_accessed=600000, transcendentals=0),
        name="square_sums",
    )(*operands)


def id_column(scalar_ref, at, count, start, rows):
    row = start + lax.broadcasted_iota(jnp.int32, (rows, LANES), 0)
    ids = jnp.zeros((rows, LANES), jnp.int32)
    for label in range(1, count):
        ids = ids + jnp.where(row >= scalar_ref[0, at + label], 1, 0)
    return ids[:, :1]


def prep_kernel(
    rank, scalar_ref, sums_ref, last_top_ref, last_bottom_ref, top_ref, bottom_ref, other_ref,
    gain_hbm, own_hbm, weight_hbm, inverse_ref, keep_ref, give_ref, shrink_ref,
    kv_ref, gain_ref, own_ref, weight_ref, sems,
):
    rows, width = inverse_ref.shape[0], top_ref.shape[1]
    model_width = gain_hbm.shape[0] * width
    chunks = sems.shape[0] - 2
    depth = width // chunks
    first = [
        pltpu.make_async_copy(gain_hbm.at[scalar_ref[0, 2]], gain_ref, sems.at[chunks]),
        pltpu.make_async_copy(own_hbm, own_ref, sems.at[chunks + 1]),
    ]
    copies = [
        pltpu.make_async_copy(
            weight_hbm.at[pl.ds(c * depth, depth)], weight_ref.at[pl.ds(c * depth, depth)], sems.at[c]
        )
        for c in range(chunks)
    ]
    for copy in first + copies:
        copy.start()
    last = jnp.concatenate([lane_sums(last_top_ref[...]), lane_sums(last_bottom_ref[...])], axis=0)
    total = jnp.sum((sums_ref[...] + last).T, axis=0, keepdims=True)
    inverse_row = lax.rsqrt(total / model_width + EPS)
    inverse = jnp.broadcast_to(inverse_row, (LANES, rows)).T
    inverse_ref[...] = inverse
    adapters = 2 * own_ref.shape[0]
    ids = id_column(scalar_ref, 3 + gain_hbm.shape[0], adapters, 0, rows)
    first[0].wait()
    block = jnp.concatenate([top_ref[...], bottom_ref[...]], axis=0).astype(F32)
    normed = (block * inverse[:, :1] * gain_ref[...]).astype(BF16)
    first[1].wait()
    shrink = jnp.zeros((rows, 3 * rank), F32)
    for side, panel_ref in enumerate((own_ref, other_ref)):
        for j in range(panel_ref.shape[0]):
            part = lax.dot_general(normed, panel_ref[j], (((1,), (1,)), ((), ())), preferred_element_type=F32)
            shrink = shrink + jnp.where(ids == scalar_ref[0, side] + j, part, 0.0)
    half = rows // 2
    packed = jnp.concatenate([shrink[:half, :rank], shrink[half:, :rank]], axis=1)
    tensor, page, _ = shrink_ref.shape
    own_rows = page - half
    for peer in range(tensor):
        shrink_ref[peer, :half] = packed
        shrink_ref[peer, half:] = shrink[peer * own_rows : (peer + 1) * own_rows, rank:]
    total = None
    for c, copy in enumerate(copies):
        copy.wait()
        part = dot(normed[:, c * depth : (c + 1) * depth], weight_ref[c * depth : (c + 1) * depth])
        total = part if total is None else total + part
    kv_ref[...] = total
    parity = scalar_ref[0, 2] % 2
    for pair in range(tensor // 2):
        keep_ref[pair] = kv_ref[pl.ds(pl.multiple_of((2 * pair + parity) * own_rows, own_rows), own_rows)]
        give_ref[pair] = pack_rows(
            kv_ref[pl.ds(pl.multiple_of((2 * pair + 1 - parity) * own_rows, own_rows), own_rows)]
        )


def prep(scalars, sums, last, local, gains, weight, own, other, rank, tensor):
    half, width = local[0].shape
    rows = 2 * half
    columns = weight.shape[1]
    chunks = 4 if width % 1024 == 0 else 1
    page = rows // 2 + rows // tensor
    return pl.pallas_call(
        functools.partial(prep_kernel, rank),
        in_specs=[SMEM] + [VMEM] * 6 + [HBM] * 3,
        out_specs=[VMEM] * 4,
        out_shape=[
            pltpu.HBM((rows, LANES), F32),
            pltpu.HBM((tensor // 2, rows // tensor, columns), F32),
            jax.ShapeDtypeStruct((tensor // 2, rows // tensor, columns + LANES), F32),
            pltpu.HBM((tensor, page, LANES), F32),
        ],
        scratch_shapes=[
            pltpu.VMEM((rows, columns), F32),
            pltpu.VMEM((1, width), F32),
            pltpu.VMEM(own.shape, BF16),
            pltpu.VMEM(weight.shape, BF16),
            pltpu.SemaphoreType.DMA((chunks + 2,)),
        ],
        compiler_params=params(),
        cost_estimate=pl.CostEstimate(flops=700000000, bytes_accessed=6000000, transcendentals=0),
        name="norm_key_value_shrink",
    )(scalars, sums, *last, *local, other, in_hbm(gains), in_hbm(own), in_hbm(weight))


def query_kernel(columns_at, scalar_ref, *refs):
    blocks = refs[:-10]
    hidden_hbm, inverse_hbm, gain_hbm, weight_hbm, out_ref, own_ref, inverse_ref, gain_ref, weight_ref, sems = refs[-10:]
    count = 1 + len(blocks) // 2
    width = own_ref.shape[1]
    slots = weight_ref.shape[0]
    order = list(range(1, count)) + [0]

    def owner(i):
        return scalar_ref[0, columns_at + order[i]]

    def fetch(i):
        return pltpu.make_async_copy(
            weight_hbm.at[pl.ds(pl.multiple_of(owner(i) * width, width), width)],
            weight_ref.at[i % slots],
            sems.at[i % slots],
        )

    small = [
        pltpu.make_async_copy(inverse_hbm, inverse_ref, sems.at[slots]),
        pltpu.make_async_copy(gain_hbm, gain_ref, sems.at[slots + 1]),
        pltpu.make_async_copy(hidden_hbm, own_ref, sems.at[slots + 2]),
    ]
    for copy in small[:2]:
        copy.start()
    for i in range(min(slots, count)):
        fetch(i).start()
    small[2].start()
    for copy in small[:2]:
        copy.wait()
    inverse = inverse_ref[:, :1]
    for i in range(count):
        gain = gain_ref[pl.ds(owner(i), 1)].reshape(1, width)
        if order[i] == 0:
            small[2].wait()
            block = own_ref[...].astype(F32)
        else:
            at = 2 * order[i] - 2
            block = jnp.concatenate([blocks[at][...], blocks[at + 1][...]], axis=0).astype(F32)
        normed = (block * inverse * gain).astype(BF16)
        fetch(i).wait()
        part = dot(normed, weight_ref[i % slots])
        out_ref[...] = part if i == 0 else out_ref[...] + part
        if i + slots < count:
            fetch(i + slots).start()


def query_products(scalars, columns_at, hidden, blocks, gains, weight, inverse):
    rows, width = hidden.shape
    columns = weight.shape[1]
    count = 1 + len(blocks)
    flat = [half for block in blocks for half in block]
    slots = min(SLOTS, count)
    return pl.pallas_call(
        functools.partial(query_kernel, columns_at),
        in_specs=[SMEM] + [VMEM] * len(flat) + [HBM] * 4,
        out_specs=VMEM,
        out_shape=jax.ShapeDtypeStruct((rows, columns), F32),
        scratch_shapes=[
            pltpu.VMEM(hidden.shape, BF16),
            pltpu.VMEM(inverse.shape, F32),
            pltpu.VMEM(gains.shape, F32),
            pltpu.VMEM((slots, width, columns), BF16),
            pltpu.SemaphoreType.DMA((slots + 3,)),
        ],
        compiler_params=params(24),
        cost_estimate=pl.CostEstimate(flops=2000000000, bytes_accessed=17000000, transcendentals=0),
        name="query_products",
    )(scalars, *flat, in_hbm(hidden), in_hbm(inverse), in_hbm(gains), in_hbm(weight))


def spread(ids, values, first, second, each):
    labels = [first + j for j in range(each)] + [second + j for j in range(each)]
    return jnp.concatenate([jnp.where(ids == label, values, 0.0) for label in labels], axis=1).astype(BF16)


def finish_kernel(
    rank, scalar_ref, parts_ref, acc_ref, up_other_ref, up_own_hbm, kv_own_hbm, kv_other_hbm,
    out_ref, kv_delta_ref, up_ref, kv_ref, sems,
):
    each = up_own_hbm.shape[0]
    copies = [
        pltpu.make_async_copy(up_own_hbm, up_ref, sems.at[0]),
        pltpu.make_async_copy(kv_own_hbm, kv_ref.at[pl.ds(0, each)], sems.at[1]),
        pltpu.make_async_copy(kv_other_hbm, kv_ref.at[pl.ds(each, each)], sems.at[2]),
    ]
    for copy in copies:
        copy.start()
    rows = out_ref.shape[0]
    half = rows // 2
    own_rows, kv_columns = kv_delta_ref.shape
    kv_width = kv_columns // 2
    columns = out_ref.shape[1]
    first, second = scalar_ref[0, 0], scalar_ref[0, 1]
    at = 3 + parts_ref.shape[0]
    ids = id_column(scalar_ref, at, 2 * each, 0, rows)
    own_ids = id_column(scalar_ref, at, 2 * each, scalar_ref[0, 2] * own_rows, own_rows)
    total = parts_ref[0]
    for peer in range(1, parts_ref.shape[0]):
        total = total + parts_ref[peer]
    shrink = jnp.concatenate([total[:half, :rank], total[:half, rank:]], axis=0)
    query_spread = spread(ids, shrink, first, second, each)
    key_spread = spread(own_ids, total[half:, :rank], first, second, each)
    value_spread = spread(own_ids, total[half:, rank:], first, second, each)
    depth = 2 * each * rank
    other_part = dot(query_spread[:, depth // 2 :], up_other_ref[...].reshape(depth // 2, columns))
    copies[0].wait()
    own_part = dot(query_spread[:, : depth // 2], up_ref[...].reshape(depth // 2, columns))
    out_ref[...] = (acc_ref[...] + own_part + other_part).astype(BF16)
    copies[1].wait()
    copies[2].wait()
    kv_delta_ref[:, :kv_width] = dot(key_spread, kv_ref[:, 0].reshape(depth, kv_width))
    kv_delta_ref[:, kv_width:] = dot(value_spread, kv_ref[:, 1].reshape(depth, kv_width))


def finish(scalars, parts, ups, kv_ups, acc, rank):
    rows = acc.shape[0]
    own_rows = rows // parts.shape[0]
    columns = ups[0].shape[2]
    kv_columns = 2 * kv_ups[0].shape[3]
    each = ups[0].shape[0]
    return pl.pallas_call(
        functools.partial(finish_kernel, rank),
        in_specs=[SMEM] + [VMEM] * 3 + [HBM] * 3,
        out_specs=[VMEM, VMEM],
        out_shape=[
            jax.ShapeDtypeStruct((rows, columns), BF16),
            jax.ShapeDtypeStruct((own_rows, kv_columns), F32),
        ],
        scratch_shapes=[
            pltpu.VMEM(ups[0].shape, BF16),
            pltpu.VMEM((2 * each,) + kv_ups[0].shape[1:], BF16),
            pltpu.SemaphoreType.DMA((3,)),
        ],
        compiler_params=params(),
        cost_estimate=pl.CostEstimate(flops=100000000, bytes_accessed=2000000, transcendentals=0),
        name="adapter_terms",
    )(scalars, parts, acc, ups[1], in_hbm(ups[0]), in_hbm(kv_ups[0]), in_hbm(kv_ups[1]))


def pair_kernel(scalar_ref, keep_ref, got_ref, *out_refs):
    index = lax.div(scalar_ref[0, 2], 2)
    for distance, out_ref in enumerate(out_refs):
        other = index ^ distance
        total = keep_ref[other] + unpack_rows(got_ref[other])
        out_ref[...] = total if distance == 0 else pack_rows(total)


def pair_sums(scalars, keep, got):
    count, own_rows, columns = keep.shape
    return pl.pallas_call(
        pair_kernel,
        in_specs=[SMEM, VMEM, VMEM],
        out_specs=[VMEM] * count,
        out_shape=[jax.ShapeDtypeStruct((own_rows, columns), F32)]
        + [jax.ShapeDtypeStruct((own_rows, columns + LANES), F32)] * (count - 1),
        compiler_params=params(),
        cost_estimate=pl.CostEstimate(flops=100000, bytes_accessed=1500000, transcendentals=0),
        name="pair_sums",
    )(scalars, in_hbm(keep), got)


def fresh_kernel(count, *refs):
    parts = refs[:count]
    delta_ref, cosine_ref, sine_ref, out_ref, heads_ref = refs[count:]
    total = parts[0][...]
    for part in parts[1:]:
        total = total + unpack_rows(part[...])
    total = total + delta_ref[...]
    kv_width = total.shape[1] // 2
    newest = jnp.concatenate(
        [rotate_heads(total[:, :kv_width], cosine_ref[...], sine_ref[...]), total[:, kv_width:]], axis=1
    ).astype(BF16)
    out_ref[:, 0, :] = newest[:, :kv_width]
    out_ref[:, 1, :] = newest[:, kv_width:]
    spread = newest.astype(F32)
    for head in range(heads_ref.shape[1]):
        heads_ref[:, head, :] = spread[:, head * HEAD_WIDTH : (head + 1) * HEAD_WIDTH]


def fresh(parts, delta, cosine, sine):
    own_rows, columns = delta.shape
    return pl.pallas_call(
        functools.partial(fresh_kernel, len(parts)),
        out_shape=[
            jax.ShapeDtypeStruct((own_rows, 2, columns // 2), BF16),
            jax.ShapeDtypeStruct((own_rows, columns // HEAD_WIDTH, HEAD_WIDTH), F32),
        ],
        compiler_params=params(),
        cost_estimate=pl.CostEstimate(flops=100000, bytes_accessed=1000000, transcendentals=0),
        name="new_key_value",
    )(*parts, delta, cosine, sine)


def attend_kernel(
    lengths_ref, query_ref, newest_ref, cosine_ref, sine_ref, cache_hbm, out_ref, query_heads_ref, scores_ref, weights_ref, fresh_ref,
    cache_ref, sems,
):
    tensor, own_rows, columns = query_ref.shape
    per_peer = columns // HEAD_WIDTH
    positions = cache_ref.shape[2]
    key_heads = cache_ref.shape[3] // HEAD_WIDTH
    heads = tensor * per_peer
    groups = heads // key_heads
    scale = 1.0 / math.sqrt(HEAD_WIDTH)
    pair = 2 * groups
    parts = sems.shape[1]
    step = own_rows // parts
    copies = [
        [
            pltpu.make_async_copy(
                cache_hbm.at[pl.ds(i * step, step), which], cache_ref.at[which, pl.ds(i * step, step)], sems.at[which, i]
            )
            for i in range(parts)
        ]
        for which in range(2)
    ]
    for copy in copies[0] + copies[1]:
        copy.start()
    for peer in range(tensor):
        part = rotate_heads(query_ref[peer].astype(F32), cosine_ref[...], sine_ref[...]).astype(BF16).astype(F32)
        for j in range(per_peer):
            query_heads_ref[:, peer * per_peer + j, :] = part[:, j * HEAD_WIDTH : (j + 1) * HEAD_WIDTH]
    side = lax.broadcasted_iota(jnp.int32, (pair, 2 * HEAD_WIDTH), 0) < groups
    on_side = side == (lax.broadcasted_iota(jnp.int32, (pair, 2 * HEAD_WIDTH), 1) < HEAD_WIDTH)
    lane = lax.broadcasted_iota(jnp.int32, (heads, positions), 1)

    def to_heads(part):
        return jnp.broadcast_to(part[:, None, :], (key_heads, groups, HEAD_WIDTH)).reshape(heads, HEAD_WIDTH)

    def score_step(row, carry):
        query = query_heads_ref[row]
        for k in range(0, key_heads, 2):
            two = query[k * groups : (k + 2) * groups]
            spread = jnp.where(on_side, jnp.concatenate([two, two], axis=1), 0.0).astype(BF16)
            keys = cache_ref[0, row, :, k * HEAD_WIDTH : (k + 2) * HEAD_WIDTH]
            scores_ref[row, k * groups : (k + 2) * groups] = lax.dot_general(
                spread, keys, (((1,), (1,)), ((), ())), preferred_element_type=F32
            )
        return carry

    def weight_step(row, carry):
        score = jnp.where(lane < lengths_ref[0, row], scores_ref[row] * scale, -1e30)
        new_key = to_heads(newest_ref[row, :key_heads])
        new_value = to_heads(newest_ref[row, key_heads:])
        new_score = jnp.sum(query_heads_ref[row] * new_key, axis=1, keepdims=True) * scale
        top = jnp.maximum(jnp.max(score, axis=1, keepdims=True), new_score)
        weights = jnp.exp(score - top)
        new_weight = jnp.exp(new_score - top)
        denominator = jnp.sum(weights, axis=1, keepdims=True) + new_weight
        weights_ref[row] = (weights / denominator).astype(BF16)
        fresh_ref[row] = (new_weight / denominator).astype(BF16).astype(F32) * new_value
        return carry

    def value_step(row, carry):
        for k in range(0, key_heads, 2):
            values = cache_ref[1, row, :, k * HEAD_WIDTH : (k + 2) * HEAD_WIDTH]
            both = dot(weights_ref[row, k * groups : (k + 2) * groups], values)
            query_heads_ref[row, k * groups : (k + 1) * groups] = (
                both[:groups, :HEAD_WIDTH] + fresh_ref[row, k * groups : (k + 1) * groups]
            )
            query_heads_ref[row, (k + 1) * groups : (k + 2) * groups] = (
                both[groups:, HEAD_WIDTH:] + fresh_ref[row, (k + 1) * groups : (k + 2) * groups]
            )
        return carry

    for i, copy in enumerate(copies[0]):
        copy.wait()
        lax.fori_loop(i * step, (i + 1) * step, score_step, 0, unroll=True)
    lax.fori_loop(0, own_rows, weight_step, 0, unroll=UNROLL)
    for i, copy in enumerate(copies[1]):
        copy.wait()
        lax.fori_loop(i * step, (i + 1) * step, value_step, 0, unroll=True)
    for head in range(heads):
        out_ref[:, head * HEAD_WIDTH : (head + 1) * HEAD_WIDTH] = query_heads_ref[:, head, :].astype(BF16)


def attend(query_rows, newest_heads, cosine, sine, cache, lengths):
    tensor, own_rows, columns = query_rows.shape
    heads = tensor * columns // HEAD_WIDTH
    return pl.pallas_call(
        attend_kernel,
        in_specs=[SMEM] + [VMEM] * 4 + [HBM],
        out_specs=VMEM,
        out_shape=jax.ShapeDtypeStruct((own_rows, tensor * columns), BF16),
        scratch_shapes=[
            pltpu.VMEM((own_rows, heads, HEAD_WIDTH), F32),
            pltpu.VMEM((own_rows, heads, cache.shape[2]), F32),
            pltpu.VMEM((own_rows, heads, cache.shape[2]), BF16),
            pltpu.VMEM((own_rows, heads, HEAD_WIDTH), F32),
            pltpu.VMEM((2, own_rows) + cache.shape[2:], BF16),
            pltpu.SemaphoreType.DMA((2, 2)),
        ],
        compiler_params=params(),
        cost_estimate=pl.CostEstimate(flops=400000000, bytes_accessed=7000000, transcendentals=100000),
        name="attention",
    )(lengths, query_rows, newest_heads, cosine, sine, in_hbm(cache))


def make_body(mesh):
    tensor = mesh.shape["tensor"]
    shards = mesh.shape["adapter"]
    order = ring_order(tensor)
    place_of = [order.index(t) for t in range(tensor)]
    right = [(order[i], order[(i + 1) % tensor]) for i in range(tensor)]
    left = [(b, a) for a, b in right]
    swap = [(i, shards - 1 - i) for i in range(shards)]

    def table(own_adapters):
        lines = []
        for side in range(shards):
            for position in range(tensor):
                place = place_of[position]
                steps = [0] + [sign * step for step in range(1, tensor // 2) for sign in (-1, 1)] + [tensor // 2]
                owners = [order[(place + step) % tensor] for step in steps]
                lines.append([side * own_adapters, (shards - 1 - side) * own_adapters, position] + owners)
        return np.array(lines, np.int32)

    def everyone(x):
        return lax.all_to_all(x, "tensor", 0, 0, tiled=True)

    def go(x, pairs):
        return lax.ppermute(x, "tensor", pairs)

    def body(
        hidden,
        input_norm_scale,
        query_weight,
        key_value_weight,
        adapter_down_weight,
        adapter_up_query,
        adapter_up_key_value,
        request_adapter,
        key_value_cache,
        lengths,
    ):
        position = lax.axis_index("tensor")
        side = lax.axis_index("adapter")
        rows, width = hidden.shape[1:]
        own_rows = rows // tensor
        half = rows // 2
        own_adapters = adapter_down_weight.shape[0]
        rank = adapter_up_query.shape[1]
        kv_width = adapter_up_key_value.shape[3]
        gains = input_norm_scale.reshape(tensor, 1, width)
        labels = jnp.arange(shards * own_adapters, dtype=jnp.int32)
        first_rows = jnp.sum((request_adapter < labels[:, None]).astype(jnp.int32), axis=1)
        scalars = jnp.concatenate(
            [
                lax.dynamic_slice_in_dim(jnp.asarray(table(own_adapters)), side * tensor + position, 1, 0),
                first_rows[None],
            ],
            axis=1,
        )
        own_down = adapter_down_weight.transpose(0, 2, 1)
        cosine, sine = rotary_tables(lengths[0])

        local = (hidden[0, :half], hidden[0, half:])
        from_left = from_right = local
        blocks = []
        sums = None
        fresh_blocks = [local]
        for step in range(1, tensor // 2):
            top_left = go(from_left[0], right)
            bottom_right = go(from_right[1], left)
            top_right = go(from_right[0], left)
            bottom_left = go(from_left[1], right)
            from_left, from_right = (top_left, bottom_left), (top_right, bottom_right)
            if step == tensor // 2 - 1:
                sums = square_sums(fresh_blocks, sums)
                fresh_blocks = []
            blocks += [from_left, from_right]
            fresh_blocks += [from_left, from_right]
        last = (go(from_left[0], right), go(from_right[1], left))
        panels = (own_down, adapter_up_query, adapter_up_key_value)

        other_down, other_up, other_kv = (lax.ppermute(w, "adapter", swap) for w in panels)
        sums = square_sums(fresh_blocks, sums)
        blocks.append(last)

        inverse, keep, give, shrink = prep(
            scalars, sums, last, local, gains, key_value_weight, own_down, other_down, rank, tensor
        )
        shrink_parts = everyone(shrink)
        acc = query_products(scalars, 3, hidden[0], blocks, gains, query_weight, inverse)
        got = go(give.astype(NARROW), [(t, t ^ 1) for t in range(tensor)])
        pair = pair_sums(scalars, keep, got.astype(F32))
        kv_parts = [pair[0]] + [
            go(pair[d].astype(NARROW), [(t, t ^ (2 * d)) for t in range(tensor)]).astype(F32)
            for d in range(1, tensor // 2)
        ]
        query, kv_delta = finish(
            scalars, shrink_parts, (adapter_up_query, other_up), (adapter_up_key_value, other_kv), acc, rank
        )
        query_rows = everyone(after(query, got).reshape(tensor, own_rows, -1))
        newest, newest_heads = fresh(kv_parts, kv_delta, cosine, sine)
        attended = attend(query_rows, newest_heads, cosine, sine, key_value_cache[0], lengths)
        return attended[None], newest[None]

    return body


def solution(mesh):
    return jax.shard_map(
        make_body(mesh),
        mesh=mesh,
        in_specs=(
            P("adapter", "group", "tensor"),
            P(),
            P(None, "tensor"),
            P("tensor", None),
            P(("group", "adapter"), "tensor", None),
            P(("group", "adapter"), None, "tensor"),
            P(("group", "adapter"), None, None, None),
            P("adapter", "group"),
            P("adapter", ("group", "tensor"), None, None, None),
            P("adapter", ("group", "tensor")),
        ),
        out_specs=(
            P("adapter", ("group", "tensor"), None),
            P("adapter", ("group", "tensor"), None, None),
        ),
        check_vma=False,
    )
```

```python
import functools
import math

import jax
import jax.numpy as jnp
import numpy as np
from jax import lax
from jax.experimental import pallas as pl
from jax.experimental.pallas import tpu as pltpu
from jax.sharding import PartitionSpec as P

HEAD_WIDTH = 128
LANES = 128
EPS = 1e-05
THETA = 500000.0
UNROLL = 4
NARROW = jnp.float16
SLOTS = 4
F32 = jnp.float32
BF16 = jnp.bfloat16


def ring_order(size):
    if size == 8:
        return [0, 2, 4, 6, 7, 5, 3, 1]
    return list(range(size))


def dot(a, b):
    return jnp.dot(a, b, preferred_element_type=F32)


def params(mib=16):
    return pltpu.CompilerParams(vmem_limit_bytes=mib * 1024 * 1024)


def after(value, *others):
    return lax.optimization_barrier((value, *others))[0]


VMEM = pl.BlockSpec(memory_space=pltpu.VMEM)
SMEM = pl.BlockSpec(memory_space=pltpu.SMEM)
HBM = pl.BlockSpec(memory_space=pltpu.HBM)


def in_hbm(value):
    return pltpu.with_memory_space_constraint(value, pltpu.HBM)


def rotary_tables(positions):
    half = HEAD_WIDTH // 2
    frequency = THETA ** (-(jnp.arange(half).astype(F32) * 2.0 / HEAD_WIDTH))
    angles = positions.astype(F32)[:, None] * frequency[None, :]
    cosine = jnp.cos(angles)
    sine = jnp.sin(angles)
    return jnp.concatenate([cosine, cosine], axis=1), jnp.concatenate([-sine, sine], axis=1)


def rotate_heads(values, cosine, sine):
    turned = []
    for head in range(values.shape[1] // HEAD_WIDTH):
        part = values[:, head * HEAD_WIDTH : (head + 1) * HEAD_WIDTH]
        turned.append(part * cosine + pltpu.roll(part, HEAD_WIDTH // 2, 1) * sine)
    return jnp.concatenate(turned, axis=1)


def pack_rows(values):
    most = jnp.max(jnp.abs(values), axis=1, keepdims=True)
    exponent = jnp.ceil(jnp.log2(jnp.maximum(most, 1e-30)))
    scaled = values * jnp.exp2(14.0 - exponent)
    return jnp.concatenate([scaled, jnp.broadcast_to(exponent, (values.shape[0], LANES))], axis=1)


def unpack_rows(values):
    width = values.shape[1] - LANES
    return values[:, :width] * jnp.exp2(values[:, width : width + 1] - 14.0)


def lane_sums(block):
    wide = block.astype(F32)
    squares = wide * wide
    lanes = squares[:, :LANES]
    for at in range(LANES, squares.shape[1], LANES):
        lanes = lanes + squares[:, at : at + LANES]
    return lanes


def sums_kernel(first, *refs):
    out_ref = refs[-1]
    half = out_ref.shape[0] // 2
    tops = refs[0:-1:2] if first else refs[0:-2:2]
    bottoms = refs[1:-1:2] if first else refs[1:-2:2]
    top = None if first else refs[-2][:half]
    bottom = None if first else refs[-2][half:]
    for top_ref, bottom_ref in zip(tops, bottoms):
        more, below = lane_sums(top_ref[...]), lane_sums(bottom_ref[...])
        top = more if top is None else top + more
        bottom = below if bottom is None else bottom + below
    out_ref[:half] = top
    out_ref[half:] = bottom


def square_sums(blocks, before):
    flat = [half for block in blocks for half in block]
    rows = 2 * flat[0].shape[0]
    operands = flat + ([] if before is None else [before])
    return pl.pallas_call(
        functools.partial(sums_kernel, before is None),
        in_specs=[VMEM] * len(operands),
        out_specs=VMEM,
        out_shape=jax.ShapeDtypeStruct((rows, LANES), F32),
        compiler_params=params(),
        cost_estimate=pl.CostEstimate(flops=1000000, bytes_accessed=600000, transcendentals=0),
        name="square_sums",
    )(*operands)


def id_column(scalar_ref, at, count, start, rows):
    row = start + lax.broadcasted_iota(jnp.int32, (rows, LANES), 0)
    ids = jnp.zeros((rows, LANES), jnp.int32)
    for label in range(1, count):
        ids = ids + jnp.where(row >= scalar_ref[0, at + label], 1, 0)
    return ids[:, :1]


def prep_kernel(
    rank, scalar_ref, sums_ref, last_top_ref, last_bottom_ref, top_ref, bottom_ref, other_ref,
    gain_hbm, own_hbm, weight_hbm, inverse_ref, keep_ref, shrink_ref, *refs,
):
    give_refs = refs[:-5]
    kv_ref, gain_ref, own_ref, weight_ref, sems = refs[-5:]
    rows, width = inverse_ref.shape[0], top_ref.shape[1]
    model_width = gain_hbm.shape[0] * width
    chunks = sems.shape[0] - 2
    depth = width // chunks
    first = [
        pltpu.make_async_copy(gain_hbm.at[scalar_ref[0, 2]], gain_ref, sems.at[chunks]),
        pltpu.make_async_copy(own_hbm, own_ref, sems.at[chunks + 1]),
    ]
    copies = [
        pltpu.make_async_copy(
            weight_hbm.at[pl.ds(c * depth, depth)], weight_ref.at[pl.ds(c * depth, depth)], sems.at[c]
        )
        for c in range(chunks)
    ]
    for copy in first + copies:
        copy.start()
    last = jnp.concatenate([lane_sums(last_top_ref[...]), lane_sums(last_bottom_ref[...])], axis=0)
    total = jnp.sum((sums_ref[...] + last).T, axis=0, keepdims=True)
    inverse_row = lax.rsqrt(total / model_width + EPS)
    inverse = jnp.broadcast_to(inverse_row, (LANES, rows)).T
    inverse_ref[...] = inverse
    adapters = 2 * own_ref.shape[0]
    ids = id_column(scalar_ref, 3 + gain_hbm.shape[0], adapters, 0, rows)
    first[0].wait()
    block = jnp.concatenate([top_ref[...], bottom_ref[...]], axis=0).astype(F32)
    normed = (block * inverse[:, :1] * gain_ref[...]).astype(BF16)
    first[1].wait()
    shrink = jnp.zeros((rows, 3 * rank), F32)
    for side, panel_ref in enumerate((own_ref, other_ref)):
        for j in range(panel_ref.shape[0]):
            part = lax.dot_general(normed, panel_ref[j], (((1,), (1,)), ((), ())), preferred_element_type=F32)
            shrink = shrink + jnp.where(ids == scalar_ref[0, side] + j, part, 0.0)
    half = rows // 2
    packed = jnp.concatenate([shrink[:half, :rank], shrink[half:, :rank]], axis=1)
    tensor, page, _ = shrink_ref.shape
    own_rows = page - half
    for peer in range(tensor):
        shrink_ref[peer, :half] = packed
        shrink_ref[peer, half:] = shrink[peer * own_rows : (peer + 1) * own_rows, rank:]
    total = None
    for c, copy in enumerate(copies):
        copy.wait()
        part = dot(normed[:, c * depth : (c + 1) * depth], weight_ref[c * depth : (c + 1) * depth])
        total = part if total is None else total + part
    kv_ref[...] = total
    index = lax.div(scalar_ref[0, 2], 2)
    both = 2 * own_rows
    keep_ref[...] = kv_ref[pl.ds(pl.multiple_of(index * both, both), both)]
    for distance, give_ref in enumerate(give_refs, 1):
        give_ref[...] = pack_rows(kv_ref[pl.ds(pl.multiple_of((index ^ distance) * both, both), both)])


def prep(scalars, sums, last, local, gains, weight, own, other, rank, tensor):
    half, width = local[0].shape
    rows = 2 * half
    columns = weight.shape[1]
    chunks = 4 if width % 1024 == 0 else 1
    page = rows // 2 + rows // tensor
    return pl.pallas_call(
        functools.partial(prep_kernel, rank),
        in_specs=[SMEM] + [VMEM] * 6 + [HBM] * 3,
        out_specs=[VMEM] * (tensor // 2 + 2),
        out_shape=[
            pltpu.HBM((rows, LANES), F32),
            pltpu.HBM((2 * rows // tensor, columns), F32),
            pltpu.HBM((tensor, page, LANES), F32),
        ]
        + [jax.ShapeDtypeStruct((2 * rows // tensor, columns + LANES), F32)] * (tensor // 2 - 1),
        scratch_shapes=[
            pltpu.VMEM((rows, columns), F32),
            pltpu.VMEM((1, width), F32),
            pltpu.VMEM(own.shape, BF16),
            pltpu.VMEM(weight.shape, BF16),
            pltpu.SemaphoreType.DMA((chunks + 2,)),
        ],
        compiler_params=params(),
        cost_estimate=pl.CostEstimate(flops=700000000, bytes_accessed=6000000, transcendentals=0),
        name="norm_key_value_shrink",
    )(scalars, sums, *last, *local, other, in_hbm(gains), in_hbm(own), in_hbm(weight))


def query_kernel(columns_at, scalar_ref, *refs):
    blocks = refs[:-10]
    hidden_hbm, inverse_hbm, gain_hbm, weight_hbm, out_ref, own_ref, inverse_ref, gain_ref, weight_ref, sems = refs[-10:]
    count = 1 + len(blocks) // 2
    width = own_ref.shape[1]
    slots = weight_ref.shape[0]
    order = list(range(1, count)) + [0]

    def owner(i):
        return scalar_ref[0, columns_at + order[i]]

    def fetch(i):
        return pltpu.make_async_copy(
            weight_hbm.at[pl.ds(pl.multiple_of(owner(i) * width, width), width)],
            weight_ref.at[i % slots],
            sems.at[i % slots],
        )

    small = [
        pltpu.make_async_copy(inverse_hbm, inverse_ref, sems.at[slots]),
        pltpu.make_async_copy(gain_hbm, gain_ref, sems.at[slots + 1]),
        pltpu.make_async_copy(hidden_hbm, own_ref, sems.at[slots + 2]),
    ]
    for copy in small[:2]:
        copy.start()
    for i in range(min(slots, count)):
        fetch(i).start()
    small[2].start()
    for copy in small[:2]:
        copy.wait()
    inverse = inverse_ref[:, :1]
    for i in range(count):
        gain = gain_ref[pl.ds(owner(i), 1)].reshape(1, width)
        if order[i] == 0:
            small[2].wait()
            block = own_ref[...].astype(F32)
        else:
            at = 2 * order[i] - 2
            block = jnp.concatenate([blocks[at][...], blocks[at + 1][...]], axis=0).astype(F32)
        normed = (block * inverse * gain).astype(BF16)
        fetch(i).wait()
        part = dot(normed, weight_ref[i % slots])
        out_ref[...] = part if i == 0 else out_ref[...] + part
        if i + slots < count:
            fetch(i + slots).start()


def query_products(scalars, columns_at, hidden, blocks, gains, weight, inverse):
    rows, width = hidden.shape
    columns = weight.shape[1]
    count = 1 + len(blocks)
    flat = [half for block in blocks for half in block]
    slots = min(SLOTS, count)
    return pl.pallas_call(
        functools.partial(query_kernel, columns_at),
        in_specs=[SMEM] + [VMEM] * len(flat) + [HBM] * 4,
        out_specs=VMEM,
        out_shape=jax.ShapeDtypeStruct((rows, columns), F32),
        scratch_shapes=[
            pltpu.VMEM(hidden.shape, BF16),
            pltpu.VMEM(inverse.shape, F32),
            pltpu.VMEM(gains.shape, F32),
            pltpu.VMEM((slots, width, columns), BF16),
            pltpu.SemaphoreType.DMA((slots + 3,)),
        ],
        compiler_params=params(24),
        cost_estimate=pl.CostEstimate(flops=2000000000, bytes_accessed=17000000, transcendentals=0),
        name="query_products",
    )(scalars, *flat, in_hbm(hidden), in_hbm(inverse), in_hbm(gains), in_hbm(weight))


def spread(ids, values, first, second, each):
    labels = [first + j for j in range(each)] + [second + j for j in range(each)]
    return jnp.concatenate([jnp.where(ids == label, values, 0.0) for label in labels], axis=1).astype(BF16)


def finish_kernel(
    rank, scalar_ref, parts_ref, acc_ref, up_other_ref, up_own_hbm, kv_own_hbm, kv_other_hbm,
    out_ref, kv_delta_ref, up_ref, kv_ref, sems,
):
    each = up_own_hbm.shape[0]
    copies = [
        pltpu.make_async_copy(up_own_hbm, up_ref, sems.at[0]),
        pltpu.make_async_copy(kv_own_hbm, kv_ref.at[pl.ds(0, each)], sems.at[1]),
        pltpu.make_async_copy(kv_other_hbm, kv_ref.at[pl.ds(each, each)], sems.at[2]),
    ]
    for copy in copies:
        copy.start()
    rows = out_ref.shape[0]
    half = rows // 2
    own_rows, kv_columns = kv_delta_ref.shape
    kv_width = kv_columns // 2
    columns = out_ref.shape[1]
    first, second = scalar_ref[0, 0], scalar_ref[0, 1]
    at = 3 + parts_ref.shape[0]
    ids = id_column(scalar_ref, at, 2 * each, 0, rows)
    own_ids = id_column(scalar_ref, at, 2 * each, scalar_ref[0, 2] * own_rows, own_rows)
    total = parts_ref[0]
    for peer in range(1, parts_ref.shape[0]):
        total = total + parts_ref[peer]
    shrink = jnp.concatenate([total[:half, :rank], total[:half, rank:]], axis=0)
    query_spread = spread(ids, shrink, first, second, each)
    key_spread = spread(own_ids, total[half:, :rank], first, second, each)
    value_spread = spread(own_ids, total[half:, rank:], first, second, each)
    depth = 2 * each * rank
    other_part = dot(query_spread[:, depth // 2 :], up_other_ref[...].reshape(depth // 2, columns))
    copies[0].wait()
    own_part = dot(query_spread[:, : depth // 2], up_ref[...].reshape(depth // 2, columns))
    out_ref[...] = (acc_ref[...] + own_part + other_part).astype(BF16)
    copies[1].wait()
    copies[2].wait()
    kv_delta_ref[:, :kv_width] = dot(key_spread, kv_ref[:, 0].reshape(depth, kv_width))
    kv_delta_ref[:, kv_width:] = dot(value_spread, kv_ref[:, 1].reshape(depth, kv_width))


def finish(scalars, parts, ups, kv_ups, acc, rank):
    rows = acc.shape[0]
    own_rows = rows // parts.shape[0]
    columns = ups[0].shape[2]
    kv_columns = 2 * kv_ups[0].shape[3]
    each = ups[0].shape[0]
    return pl.pallas_call(
        functools.partial(finish_kernel, rank),
        in_specs=[SMEM] + [VMEM] * 3 + [HBM] * 3,
        out_specs=[VMEM, VMEM],
        out_shape=[
            jax.ShapeDtypeStruct((rows, columns), BF16),
            jax.ShapeDtypeStruct((own_rows, kv_columns), F32),
        ],
        scratch_shapes=[
            pltpu.VMEM(ups[0].shape, BF16),
            pltpu.VMEM((2 * each,) + kv_ups[0].shape[1:], BF16),
            pltpu.SemaphoreType.DMA((3,)),
        ],
        compiler_params=params(),
        cost_estimate=pl.CostEstimate(flops=100000000, bytes_accessed=2000000, transcendentals=0),
        name="adapter_terms",
    )(scalars, parts, acc, ups[1], in_hbm(ups[0]), in_hbm(kv_ups[0]), in_hbm(kv_ups[1]))


def line_kernel(scalar_ref, keep_ref, *refs):
    got_refs, (mine_ref, give_ref, total_ref) = refs[:-3], refs[-3:]
    own_rows = mine_ref.shape[0]
    total = keep_ref[...]
    for got_ref in got_refs:
        total = total + unpack_rows(got_ref[...])
    total_ref[...] = total
    parity = scalar_ref[0, 2] % 2
    mine_ref[...] = total_ref[pl.ds(pl.multiple_of(parity * own_rows, own_rows), own_rows)]
    give_ref[...] = pack_rows(total_ref[pl.ds(pl.multiple_of((1 - parity) * own_rows, own_rows), own_rows)])


def line_sums(scalars, keep, got):
    both, columns = keep.shape
    return pl.pallas_call(
        line_kernel,
        in_specs=[SMEM] + [VMEM] * (1 + len(got)),
        out_specs=[VMEM] * 2,
        out_shape=[
            jax.ShapeDtypeStruct((both // 2, columns), F32),
            jax.ShapeDtypeStruct((both // 2, columns + LANES), F32),
        ],
        scratch_shapes=[pltpu.VMEM(keep.shape, F32)],
        compiler_params=params(),
        cost_estimate=pl.CostEstimate(flops=100000, bytes_accessed=1500000, transcendentals=0),
        name="line_sums",
    )(scalars, in_hbm(keep), *got)


def fresh_kernel(count, *refs):
    parts = refs[:count]
    delta_ref, cosine_ref, sine_ref, out_ref, heads_ref = refs[count:]
    total = parts[0][...]
    for part in parts[1:]:
        total = total + unpack_rows(part[...])
    total = total + delta_ref[...]
    kv_width = total.shape[1] // 2
    newest = jnp.concatenate(
        [rotate_heads(total[:, :kv_width], cosine_ref[...], sine_ref[...]), total[:, kv_width:]], axis=1
    ).astype(BF16)
    out_ref[:, 0, :] = newest[:, :kv_width]
    out_ref[:, 1, :] = newest[:, kv_width:]
    spread = newest.astype(F32)
    for head in range(heads_ref.shape[1]):
        heads_ref[:, head, :] = spread[:, head * HEAD_WIDTH : (head + 1) * HEAD_WIDTH]


def fresh(parts, delta, cosine, sine):
    own_rows, columns = delta.shape
    return pl.pallas_call(
        functools.partial(fresh_kernel, len(parts)),
        out_shape=[
            jax.ShapeDtypeStruct((own_rows, 2, columns // 2), BF16),
            jax.ShapeDtypeStruct((own_rows, columns // HEAD_WIDTH, HEAD_WIDTH), F32),
        ],
        compiler_params=params(),
        cost_estimate=pl.CostEstimate(flops=100000, bytes_accessed=1000000, transcendentals=0),
        name="new_key_value",
    )(*parts, delta, cosine, sine)


def attend_kernel(
    lengths_ref, query_ref, newest_ref, cosine_ref, sine_ref, cache_hbm, out_ref, query_heads_ref, scores_ref, weights_ref, fresh_ref,
    cache_ref, sems,
):
    tensor, own_rows, columns = query_ref.shape
    per_peer = columns // HEAD_WIDTH
    positions = cache_ref.shape[2]
    key_heads = cache_ref.shape[3] // HEAD_WIDTH
    heads = tensor * per_peer
    groups = heads // key_heads
    scale = 1.0 / math.sqrt(HEAD_WIDTH)
    pair = 2 * groups
    parts = sems.shape[1]
    step = own_rows // parts
    copies = [
        [
            pltpu.make_async_copy(
                cache_hbm.at[pl.ds(i * step, step), which], cache_ref.at[which, pl.ds(i * step, step)], sems.at[which, i]
            )
            for i in range(parts)
        ]
        for which in range(2)
    ]
    for copy in copies[0] + copies[1]:
        copy.start()
    for peer in range(tensor):
        part = rotate_heads(query_ref[peer].astype(F32), cosine_ref[...], sine_ref[...]).astype(BF16).astype(F32)
        for j in range(per_peer):
            query_heads_ref[:, peer * per_peer + j, :] = part[:, j * HEAD_WIDTH : (j + 1) * HEAD_WIDTH]
    side = lax.broadcasted_iota(jnp.int32, (pair, 2 * HEAD_WIDTH), 0) < groups
    on_side = side == (lax.broadcasted_iota(jnp.int32, (pair, 2 * HEAD_WIDTH), 1) < HEAD_WIDTH)
    lane = lax.broadcasted_iota(jnp.int32, (heads, positions), 1)

    def to_heads(part):
        return jnp.broadcast_to(part[:, None, :], (key_heads, groups, HEAD_WIDTH)).reshape(heads, HEAD_WIDTH)

    def score_step(row, carry):
        query = query_heads_ref[row]
        for k in range(0, key_heads, 2):
            two = query[k * groups : (k + 2) * groups]
            spread = jnp.where(on_side, jnp.concatenate([two, two], axis=1), 0.0).astype(BF16)
            keys = cache_ref[0, row, :, k * HEAD_WIDTH : (k + 2) * HEAD_WIDTH]
            scores_ref[row, k * groups : (k + 2) * groups] = lax.dot_general(
                spread, keys, (((1,), (1,)), ((), ())), preferred_element_type=F32
            )
        return carry

    def weight_step(row, carry):
        score = jnp.where(lane < lengths_ref[0, row], scores_ref[row] * scale, -1e30)
        new_key = to_heads(newest_ref[row, :key_heads])
        new_value = to_heads(newest_ref[row, key_heads:])
        new_score = jnp.sum(query_heads_ref[row] * new_key, axis=1, keepdims=True) * scale
        top = jnp.maximum(jnp.max(score, axis=1, keepdims=True), new_score)
        weights = jnp.exp(score - top)
        new_weight = jnp.exp(new_score - top)
        denominator = jnp.sum(weights, axis=1, keepdims=True) + new_weight
        weights_ref[row] = (weights / denominator).astype(BF16)
        fresh_ref[row] = (new_weight / denominator).astype(BF16).astype(F32) * new_value
        return carry

    def value_step(row, carry):
        for k in range(0, key_heads, 2):
            values = cache_ref[1, row, :, k * HEAD_WIDTH : (k + 2) * HEAD_WIDTH]
            both = dot(weights_ref[row, k * groups : (k + 2) * groups], values)
            query_heads_ref[row, k * groups : (k + 1) * groups] = (
                both[:groups, :HEAD_WIDTH] + fresh_ref[row, k * groups : (k + 1) * groups]
            )
            query_heads_ref[row, (k + 1) * groups : (k + 2) * groups] = (
                both[groups:, HEAD_WIDTH:] + fresh_ref[row, (k + 1) * groups : (k + 2) * groups]
            )
        return carry

    for i, copy in enumerate(copies[0]):
        copy.wait()
        lax.fori_loop(i * step, (i + 1) * step, score_step, 0, unroll=True)
    lax.fori_loop(0, own_rows, weight_step, 0, unroll=UNROLL)
    for i, copy in enumerate(copies[1]):
        copy.wait()
        lax.fori_loop(i * step, (i + 1) * step, value_step, 0, unroll=True)
    for head in range(heads):
        out_ref[:, head * HEAD_WIDTH : (head + 1) * HEAD_WIDTH] = query_heads_ref[:, head, :].astype(BF16)


def attend(query_rows, newest_heads, cosine, sine, cache, lengths):
    tensor, own_rows, columns = query_rows.shape
    heads = tensor * columns // HEAD_WIDTH
    return pl.pallas_call(
        attend_kernel,
        in_specs=[SMEM] + [VMEM] * 4 + [HBM],
        out_specs=VMEM,
        out_shape=jax.ShapeDtypeStruct((own_rows, tensor * columns), BF16),
        scratch_shapes=[
            pltpu.VMEM((own_rows, heads, HEAD_WIDTH), F32),
            pltpu.VMEM((own_rows, heads, cache.shape[2]), F32),
            pltpu.VMEM((own_rows, heads, cache.shape[2]), BF16),
            pltpu.VMEM((own_rows, heads, HEAD_WIDTH), F32),
            pltpu.VMEM((2, own_rows) + cache.shape[2:], BF16),
            pltpu.SemaphoreType.DMA((2, 2)),
        ],
        compiler_params=params(),
        cost_estimate=pl.CostEstimate(flops=400000000, bytes_accessed=7000000, transcendentals=100000),
        name="attention",
    )(lengths, query_rows, newest_heads, cosine, sine, in_hbm(cache))


def make_body(mesh):
    tensor = mesh.shape["tensor"]
    shards = mesh.shape["adapter"]
    order = ring_order(tensor)
    place_of = [order.index(t) for t in range(tensor)]
    right = [(order[i], order[(i + 1) % tensor]) for i in range(tensor)]
    left = [(b, a) for a, b in right]
    swap = [(i, shards - 1 - i) for i in range(shards)]

    def table(own_adapters):
        lines = []
        for side in range(shards):
            for position in range(tensor):
                place = place_of[position]
                steps = [0] + [sign * step for step in range(1, tensor // 2) for sign in (-1, 1)] + [tensor // 2]
                owners = [order[(place + step) % tensor] for step in steps]
                lines.append([side * own_adapters, (shards - 1 - side) * own_adapters, position] + owners)
        return np.array(lines, np.int32)

    def everyone(x):
        return lax.all_to_all(x, "tensor", 0, 0, tiled=True)

    def go(x, pairs):
        return lax.ppermute(x, "tensor", pairs)

    def body(
        hidden,
        input_norm_scale,
        query_weight,
        key_value_weight,
        adapter_down_weight,
        adapter_up_query,
        adapter_up_key_value,
        request_adapter,
        key_value_cache,
        lengths,
    ):
        position = lax.axis_index("tensor")
        side = lax.axis_index("adapter")
        rows, width = hidden.shape[1:]
        own_rows = rows // tensor
        half = rows // 2
        own_adapters = adapter_down_weight.shape[0]
        rank = adapter_up_query.shape[1]
        kv_width = adapter_up_key_value.shape[3]
        gains = input_norm_scale.reshape(tensor, 1, width)
        labels = jnp.arange(shards * own_adapters, dtype=jnp.int32)
        first_rows = jnp.sum((request_adapter < labels[:, None]).astype(jnp.int32), axis=1)
        scalars = jnp.concatenate(
            [
                lax.dynamic_slice_in_dim(jnp.asarray(table(own_adapters)), side * tensor + position, 1, 0),
                first_rows[None],
            ],
            axis=1,
        )
        own_down = adapter_down_weight.transpose(0, 2, 1)
        cosine, sine = rotary_tables(lengths[0])

        local = (hidden[0, :half], hidden[0, half:])
        from_left = from_right = local
        blocks = []
        sums = None
        fresh_blocks = [local]
        for step in range(1, tensor // 2):
            top_left = go(from_left[0], right)
            bottom_right = go(from_right[1], left)
            top_right = go(from_right[0], left)
            bottom_left = go(from_left[1], right)
            from_left, from_right = (top_left, bottom_left), (top_right, bottom_right)
            if step == tensor // 2 - 1:
                sums = square_sums(fresh_blocks, sums)
                fresh_blocks = []
            blocks += [from_left, from_right]
            fresh_blocks += [from_left, from_right]
        last = (go(from_left[0], right), go(from_right[1], left))
        panels = (own_down, adapter_up_query, adapter_up_key_value)

        other_down, other_up, other_kv = (lax.ppermute(w, "adapter", swap) for w in panels)
        sums = square_sums(fresh_blocks, sums)
        blocks.append(last)

        inverse, keep, shrink, *gives = prep(
            scalars, sums, last, local, gains, key_value_weight, own_down, other_down, rank, tensor
        )
        gives = [give.astype(NARROW) for give in gives]
        shrink_parts = everyone(after(shrink, *gives))
        acc = query_products(scalars, 3, hidden[0], blocks, gains, query_weight, inverse)
        got = [
            go(give, [(t, t ^ (2 * d)) for t in range(tensor)]) for d, give in enumerate(gives, 1)
        ]
        mine, give = line_sums(scalars, keep, [part.astype(F32) for part in got])
        kv_parts = [mine, go(give.astype(NARROW), [(t, t ^ 1) for t in range(tensor)]).astype(F32)]
        query, kv_delta = finish(
            scalars, shrink_parts, (adapter_up_query, other_up), (adapter_up_key_value, other_kv), acc, rank
        )
        query_rows = everyone(after(query, *got).reshape(tensor, own_rows, -1))
        newest, newest_heads = fresh(kv_parts, kv_delta, cosine, sine)
        attended = attend(query_rows, newest_heads, cosine, sine, key_value_cache[0], lengths)
        return attended[None], newest[None]

    return body


def solution(mesh):
    return jax.shard_map(
        make_body(mesh),
        mesh=mesh,
        in_specs=(
            P("adapter", "group", "tensor"),
            P(),
            P(None, "tensor"),
            P("tensor", None),
            P(("group", "adapter"), "tensor", None),
            P(("group", "adapter"), None, "tensor"),
            P(("group", "adapter"), None, None, None),
            P("adapter", "group"),
            P("adapter", ("group", "tensor"), None, None, None),
            P("adapter", ("group", "tensor")),
        ),
        out_specs=(
            P("adapter", ("group", "tensor"), None),
            P("adapter", ("group", "tensor"), None, None),
        ),
        check_vma=False,
    )
```

```python
import functools
import math

import jax
import jax.numpy as jnp
import numpy as np
from jax import lax
from jax.experimental import pallas as pl
from jax.experimental.pallas import tpu as pltpu
from jax.sharding import PartitionSpec as P

HEAD_WIDTH = 128
LANES = 128
EPS = 1e-05
THETA = 500000.0
UNROLL = 4
NARROW = jnp.float16
SLOTS = 4
F32 = jnp.float32
BF16 = jnp.bfloat16


def ring_order(size):
    if size == 8:
        return [0, 2, 4, 6, 7, 5, 3, 1]
    return list(range(size))


def dot(a, b):
    return jnp.dot(a, b, preferred_element_type=F32)


def params(mib=16):
    return pltpu.CompilerParams(vmem_limit_bytes=mib * 1024 * 1024)


def after(value, *others):
    return lax.optimization_barrier((value, *others))[0]


VMEM = pl.BlockSpec(memory_space=pltpu.VMEM)
SMEM = pl.BlockSpec(memory_space=pltpu.SMEM)
HBM = pl.BlockSpec(memory_space=pltpu.HBM)


def in_hbm(value):
    return pltpu.with_memory_space_constraint(value, pltpu.HBM)


def rotary_tables(positions):
    half = HEAD_WIDTH // 2
    frequency = THETA ** (-(jnp.arange(half).astype(F32) * 2.0 / HEAD_WIDTH))
    angles = positions.astype(F32)[:, None] * frequency[None, :]
    cosine = jnp.cos(angles)
    sine = jnp.sin(angles)
    return jnp.concatenate([cosine, cosine], axis=1), jnp.concatenate([-sine, sine], axis=1)


def rotate_heads(values, cosine, sine):
    turned = []
    for head in range(values.shape[1] // HEAD_WIDTH):
        part = values[:, head * HEAD_WIDTH : (head + 1) * HEAD_WIDTH]
        turned.append(part * cosine + pltpu.roll(part, HEAD_WIDTH // 2, 1) * sine)
    return jnp.concatenate(turned, axis=1)


def pack_rows(values):
    most = jnp.max(jnp.abs(values), axis=1, keepdims=True)
    exponent = jnp.ceil(jnp.log2(jnp.maximum(most, 1e-30)))
    scaled = values * jnp.exp2(14.0 - exponent)
    return jnp.concatenate([scaled, jnp.broadcast_to(exponent, (values.shape[0], LANES))], axis=1)


def unpack_rows(values):
    width = values.shape[1] - LANES
    return values[:, :width] * jnp.exp2(values[:, width : width + 1] - 14.0)


def lane_sums(block):
    wide = block.astype(F32)
    squares = wide * wide
    lanes = squares[:, :LANES]
    for at in range(LANES, squares.shape[1], LANES):
        lanes = lanes + squares[:, at : at + LANES]
    return lanes


def sums_kernel(first, *refs):
    out_ref = refs[-1]
    half = out_ref.shape[0] // 2
    tops = refs[0:-1:2] if first else refs[0:-2:2]
    bottoms = refs[1:-1:2] if first else refs[1:-2:2]
    top = None if first else refs[-2][:half]
    bottom = None if first else refs[-2][half:]
    for top_ref, bottom_ref in zip(tops, bottoms):
        more, below = lane_sums(top_ref[...]), lane_sums(bottom_ref[...])
        top = more if top is None else top + more
        bottom = below if bottom is None else bottom + below
    out_ref[:half] = top
    out_ref[half:] = bottom


def square_sums(blocks, before):
    flat = [half for block in blocks for half in block]
    rows = 2 * flat[0].shape[0]
    operands = flat + ([] if before is None else [before])
    return pl.pallas_call(
        functools.partial(sums_kernel, before is None),
        in_specs=[VMEM] * len(operands),
        out_specs=VMEM,
        out_shape=jax.ShapeDtypeStruct((rows, LANES), F32),
        compiler_params=params(),
        cost_estimate=pl.CostEstimate(flops=1000000, bytes_accessed=600000, transcendentals=0),
        name="square_sums",
    )(*operands)


def id_column(scalar_ref, at, count, start, rows):
    row = start + lax.broadcasted_iota(jnp.int32, (rows, LANES), 0)
    ids = jnp.zeros((rows, LANES), jnp.int32)
    for label in range(1, count):
        ids = ids + jnp.where(row >= scalar_ref[0, at + label], 1, 0)
    return ids[:, :1]


def prep_kernel(
    rank, scalar_ref, sums_ref, last_top_ref, last_bottom_ref, top_ref, bottom_ref, other_ref,
    gain_hbm, own_hbm, weight_hbm, inverse_ref, keep_ref, shrink_ref, *refs,
):
    give_refs = refs[:-5]
    kv_ref, gain_ref, own_ref, weight_ref, sems = refs[-5:]
    rows, width = inverse_ref.shape[0], top_ref.shape[1]
    model_width = gain_hbm.shape[0] * width
    chunks = sems.shape[0] - 2
    depth = width // chunks
    first = [
        pltpu.make_async_copy(gain_hbm.at[scalar_ref[0, 2]], gain_ref, sems.at[chunks]),
        pltpu.make_async_copy(own_hbm, own_ref, sems.at[chunks + 1]),
    ]
    copies = [
        pltpu.make_async_copy(
            weight_hbm.at[pl.ds(c * depth, depth)], weight_ref.at[pl.ds(c * depth, depth)], sems.at[c]
        )
        for c in range(chunks)
    ]
    for copy in first + copies:
        copy.start()
    last = jnp.concatenate([lane_sums(last_top_ref[...]), lane_sums(last_bottom_ref[...])], axis=0)
    total = jnp.sum((sums_ref[...] + last).T, axis=0, keepdims=True)
    inverse_row = lax.rsqrt(total / model_width + EPS)
    inverse = jnp.broadcast_to(inverse_row, (LANES, rows)).T
    inverse_ref[...] = inverse
    adapters = 2 * own_ref.shape[0]
    ids = id_column(scalar_ref, 3 + gain_hbm.shape[0], adapters, 0, rows)
    first[0].wait()
    block = jnp.concatenate([top_ref[...], bottom_ref[...]], axis=0).astype(F32)
    normed = (block * inverse[:, :1] * gain_ref[...]).astype(BF16)
    first[1].wait()
    shrink = jnp.zeros((rows, 3 * rank), F32)
    for side, panel_ref in enumerate((own_ref, other_ref)):
        for j in range(panel_ref.shape[0]):
            part = lax.dot_general(normed, panel_ref[j], (((1,), (1,)), ((), ())), preferred_element_type=F32)
            shrink = shrink + jnp.where(ids == scalar_ref[0, side] + j, part, 0.0)
    half = rows // 2
    packed = jnp.concatenate([shrink[:half, :rank], shrink[half:, :rank]], axis=1)
    tensor, page, _ = shrink_ref.shape
    own_rows = page - half
    for peer in range(tensor):
        shrink_ref[peer, :half] = packed
        shrink_ref[peer, half:] = shrink[peer * own_rows : (peer + 1) * own_rows, rank:]
    total = None
    for c, copy in enumerate(copies):
        copy.wait()
        part = dot(normed[:, c * depth : (c + 1) * depth], weight_ref[c * depth : (c + 1) * depth])
        total = part if total is None else total + part
    kv_ref[...] = total
    index = lax.div(scalar_ref[0, 2], 2)
    both = 2 * own_rows
    keep_ref[...] = kv_ref[pl.ds(pl.multiple_of(index * both, both), both)]
    for distance, give_ref in enumerate(give_refs, 1):
        give_ref[...] = pack_rows(kv_ref[pl.ds(pl.multiple_of((index ^ distance) * both, both), both)])


def prep(scalars, sums, last, local, gains, weight, own, other, rank, tensor):
    half, width = local[0].shape
    rows = 2 * half
    columns = weight.shape[1]
    chunks = 4 if width % 1024 == 0 else 1
    page = rows // 2 + rows // tensor
    return pl.pallas_call(
        functools.partial(prep_kernel, rank),
        in_specs=[SMEM] + [VMEM] * 6 + [HBM] * 3,
        out_specs=[VMEM] * (tensor // 2 + 2),
        out_shape=[
            pltpu.HBM((rows, LANES), F32),
            pltpu.HBM((2 * rows // tensor, columns), F32),
            pltpu.HBM((tensor, page, LANES), F32),
        ]
        + [jax.ShapeDtypeStruct((2 * rows // tensor, columns + LANES), F32)] * (tensor // 2 - 1),
        scratch_shapes=[
            pltpu.VMEM((rows, columns), F32),
            pltpu.VMEM((1, width), F32),
            pltpu.VMEM(own.shape, BF16),
            pltpu.VMEM(weight.shape, BF16),
            pltpu.SemaphoreType.DMA((chunks + 2,)),
        ],
        compiler_params=params(),
        cost_estimate=pl.CostEstimate(flops=700000000, bytes_accessed=6000000, transcendentals=0),
        name="norm_key_value_shrink",
    )(scalars, sums, *last, *local, other, in_hbm(gains), in_hbm(own), in_hbm(weight))


def query_kernel(columns_at, scalar_ref, *refs):
    blocks = refs[:-10]
    hidden_hbm, inverse_hbm, gain_hbm, weight_hbm, out_ref, own_ref, inverse_ref, gain_ref, weight_ref, sems = refs[-10:]
    count = 1 + len(blocks) // 2
    width = own_ref.shape[1]
    slots = weight_ref.shape[0]
    order = list(range(1, count)) + [0]

    def owner(i):
        return scalar_ref[0, columns_at + order[i]]

    def fetch(i):
        return pltpu.make_async_copy(
            weight_hbm.at[pl.ds(pl.multiple_of(owner(i) * width, width), width)],
            weight_ref.at[i % slots],
            sems.at[i % slots],
        )

    small = [
        pltpu.make_async_copy(inverse_hbm, inverse_ref, sems.at[slots]),
        pltpu.make_async_copy(gain_hbm, gain_ref, sems.at[slots + 1]),
        pltpu.make_async_copy(hidden_hbm, own_ref, sems.at[slots + 2]),
    ]
    for copy in small[:2]:
        copy.start()
    for i in range(min(slots, count)):
        fetch(i).start()
    small[2].start()
    for copy in small[:2]:
        copy.wait()
    inverse = inverse_ref[:, :1]
    for i in range(count):
        gain = gain_ref[pl.ds(owner(i), 1)].reshape(1, width)
        if order[i] == 0:
            small[2].wait()
            block = own_ref[...].astype(F32)
        else:
            at = 2 * order[i] - 2
            block = jnp.concatenate([blocks[at][...], blocks[at + 1][...]], axis=0).astype(F32)
        normed = (block * inverse * gain).astype(BF16)
        fetch(i).wait()
        part = dot(normed, weight_ref[i % slots])
        out_ref[...] = part if i == 0 else out_ref[...] + part
        if i + slots < count:
            fetch(i + slots).start()


def query_products(scalars, columns_at, hidden, blocks, gains, weight, inverse):
    rows, width = hidden.shape
    columns = weight.shape[1]
    count = 1 + len(blocks)
    flat = [half for block in blocks for half in block]
    slots = min(SLOTS, count)
    return pl.pallas_call(
        functools.partial(query_kernel, columns_at),
        in_specs=[SMEM] + [VMEM] * len(flat) + [HBM] * 4,
        out_specs=VMEM,
        out_shape=jax.ShapeDtypeStruct((rows, columns), F32),
        scratch_shapes=[
            pltpu.VMEM(hidden.shape, BF16),
            pltpu.VMEM(inverse.shape, F32),
            pltpu.VMEM(gains.shape, F32),
            pltpu.VMEM((slots, width, columns), BF16),
            pltpu.SemaphoreType.DMA((slots + 3,)),
        ],
        compiler_params=params(24),
        cost_estimate=pl.CostEstimate(flops=2000000000, bytes_accessed=17000000, transcendentals=0),
        name="query_products",
    )(scalars, *flat, in_hbm(hidden), in_hbm(inverse), in_hbm(gains), in_hbm(weight))


def spread(ids, values, first, second, each):
    labels = [first + j for j in range(each)] + [second + j for j in range(each)]
    return jnp.concatenate([jnp.where(ids == label, values, 0.0) for label in labels], axis=1).astype(BF16)


def finish_kernel(
    rank, scalar_ref, parts_ref, acc_ref, up_other_ref, up_own_hbm, kv_own_hbm, kv_other_hbm,
    out_ref, kv_delta_ref, up_ref, kv_ref, sems,
):
    each = up_own_hbm.shape[0]
    copies = [
        pltpu.make_async_copy(up_own_hbm, up_ref, sems.at[0]),
        pltpu.make_async_copy(kv_own_hbm, kv_ref.at[pl.ds(0, each)], sems.at[1]),
        pltpu.make_async_copy(kv_other_hbm, kv_ref.at[pl.ds(each, each)], sems.at[2]),
    ]
    for copy in copies:
        copy.start()
    rows = out_ref.shape[0]
    half = rows // 2
    own_rows, kv_columns = kv_delta_ref.shape
    kv_width = kv_columns // 2
    columns = out_ref.shape[1]
    first, second = scalar_ref[0, 0], scalar_ref[0, 1]
    at = 3 + parts_ref.shape[0]
    ids = id_column(scalar_ref, at, 2 * each, 0, rows)
    own_ids = id_column(scalar_ref, at, 2 * each, scalar_ref[0, 2] * own_rows, own_rows)
    total = parts_ref[0]
    for peer in range(1, parts_ref.shape[0]):
        total = total + parts_ref[peer]
    shrink = jnp.concatenate([total[:half, :rank], total[:half, rank:]], axis=0)
    query_spread = spread(ids, shrink, first, second, each)
    key_spread = spread(own_ids, total[half:, :rank], first, second, each)
    value_spread = spread(own_ids, total[half:, rank:], first, second, each)
    depth = 2 * each * rank
    other_part = dot(query_spread[:, depth // 2 :], up_other_ref[...].reshape(depth // 2, columns))
    copies[0].wait()
    own_part = dot(query_spread[:, : depth // 2], up_ref[...].reshape(depth // 2, columns))
    out_ref[...] = (acc_ref[...] + own_part + other_part).astype(BF16)
    copies[1].wait()
    copies[2].wait()
    kv_delta_ref[:, :kv_width] = dot(key_spread, kv_ref[:, 0].reshape(depth, kv_width))
    kv_delta_ref[:, kv_width:] = dot(value_spread, kv_ref[:, 1].reshape(depth, kv_width))


def finish(scalars, parts, ups, kv_ups, acc, rank):
    rows = acc.shape[0]
    own_rows = rows // parts.shape[0]
    columns = ups[0].shape[2]
    kv_columns = 2 * kv_ups[0].shape[3]
    each = ups[0].shape[0]
    return pl.pallas_call(
        functools.partial(finish_kernel, rank),
        in_specs=[SMEM] + [VMEM] * 3 + [HBM] * 3,
        out_specs=[VMEM, VMEM],
        out_shape=[
            jax.ShapeDtypeStruct((rows, columns), BF16),
            jax.ShapeDtypeStruct((own_rows, kv_columns), F32),
        ],
        scratch_shapes=[
            pltpu.VMEM(ups[0].shape, BF16),
            pltpu.VMEM((2 * each,) + kv_ups[0].shape[1:], BF16),
            pltpu.SemaphoreType.DMA((3,)),
        ],
        compiler_params=params(),
        cost_estimate=pl.CostEstimate(flops=100000000, bytes_accessed=2000000, transcendentals=0),
        name="adapter_terms",
    )(scalars, parts, acc, ups[1], in_hbm(ups[0]), in_hbm(kv_ups[0]), in_hbm(kv_ups[1]))


def line_kernel(scalar_ref, keep_ref, *refs):
    got_refs, (mine_ref, give_ref, total_ref) = refs[:-3], refs[-3:]
    own_rows = mine_ref.shape[0]
    total = keep_ref[...]
    for got_ref in got_refs:
        total = total + unpack_rows(got_ref[...])
    total_ref[...] = total
    parity = scalar_ref[0, 2] % 2
    mine_ref[...] = total_ref[pl.ds(pl.multiple_of(parity * own_rows, own_rows), own_rows)]
    give_ref[...] = pack_rows(total_ref[pl.ds(pl.multiple_of((1 - parity) * own_rows, own_rows), own_rows)])


def line_sums(scalars, keep, got):
    both, columns = keep.shape
    return pl.pallas_call(
        line_kernel,
        in_specs=[SMEM] + [VMEM] * (1 + len(got)),
        out_specs=[VMEM] * 2,
        out_shape=[
            jax.ShapeDtypeStruct((both // 2, columns), F32),
            jax.ShapeDtypeStruct((both // 2, columns + LANES), F32),
        ],
        scratch_shapes=[pltpu.VMEM(keep.shape, F32)],
        compiler_params=params(),
        cost_estimate=pl.CostEstimate(flops=100000, bytes_accessed=1500000, transcendentals=0),
        name="line_sums",
    )(scalars, in_hbm(keep), *got)


def fresh_kernel(count, *refs):
    parts = refs[:count]
    delta_ref, cosine_ref, sine_ref, out_ref, heads_ref = refs[count:]
    total = parts[0][...]
    for part in parts[1:]:
        total = total + unpack_rows(part[...])
    total = total + delta_ref[...]
    kv_width = total.shape[1] // 2
    newest = jnp.concatenate(
        [rotate_heads(total[:, :kv_width], cosine_ref[...], sine_ref[...]), total[:, kv_width:]], axis=1
    ).astype(BF16)
    out_ref[:, 0, :] = newest[:, :kv_width]
    out_ref[:, 1, :] = newest[:, kv_width:]
    spread = newest.astype(F32)
    for head in range(heads_ref.shape[1]):
        heads_ref[:, head, :] = spread[:, head * HEAD_WIDTH : (head + 1) * HEAD_WIDTH]


def fresh(parts, delta, cosine, sine):
    own_rows, columns = delta.shape
    return pl.pallas_call(
        functools.partial(fresh_kernel, len(parts)),
        out_shape=[
            jax.ShapeDtypeStruct((own_rows, 2, columns // 2), BF16),
            jax.ShapeDtypeStruct((own_rows, columns // HEAD_WIDTH, HEAD_WIDTH), F32),
        ],
        compiler_params=params(),
        cost_estimate=pl.CostEstimate(flops=100000, bytes_accessed=1000000, transcendentals=0),
        name="new_key_value",
    )(*parts, delta, cosine, sine)


def attend_kernel(
    lengths_ref, query_ref, newest_ref, cosine_ref, sine_ref, cache_hbm, out_ref, query_heads_ref, scores_ref, weights_ref, fresh_ref,
    cache_ref, sems,
):
    tensor, own_rows, columns = query_ref.shape
    per_peer = columns // HEAD_WIDTH
    positions = cache_ref.shape[2]
    key_heads = cache_ref.shape[3] // HEAD_WIDTH
    heads = tensor * per_peer
    groups = heads // key_heads
    scale = 1.0 / math.sqrt(HEAD_WIDTH)
    pair = 2 * groups
    parts = sems.shape[1]
    step = own_rows // parts
    copies = [
        [
            pltpu.make_async_copy(
                cache_hbm.at[pl.ds(i * step, step), which], cache_ref.at[which, pl.ds(i * step, step)], sems.at[which, i]
            )
            for i in range(parts)
        ]
        for which in range(2)
    ]
    for copy in copies[0] + copies[1]:
        copy.start()
    for peer in range(tensor):
        part = rotate_heads(query_ref[peer].astype(F32), cosine_ref[...], sine_ref[...]).astype(BF16).astype(F32)
        for j in range(per_peer):
            query_heads_ref[:, peer * per_peer + j, :] = part[:, j * HEAD_WIDTH : (j + 1) * HEAD_WIDTH]
    side = lax.broadcasted_iota(jnp.int32, (pair, 2 * HEAD_WIDTH), 0) < groups
    on_side = side == (lax.broadcasted_iota(jnp.int32, (pair, 2 * HEAD_WIDTH), 1) < HEAD_WIDTH)
    lane = lax.broadcasted_iota(jnp.int32, (heads, positions), 1)

    def to_heads(part):
        return jnp.broadcast_to(part[:, None, :], (key_heads, groups, HEAD_WIDTH)).reshape(heads, HEAD_WIDTH)

    def score_step(row, carry):
        query = query_heads_ref[row]
        for k in range(0, key_heads, 2):
            two = query[k * groups : (k + 2) * groups]
            spread = jnp.where(on_side, jnp.concatenate([two, two], axis=1), 0.0).astype(BF16)
            keys = cache_ref[0, row, :, k * HEAD_WIDTH : (k + 2) * HEAD_WIDTH]
            scores_ref[row, k * groups : (k + 2) * groups] = lax.dot_general(
                spread, keys, (((1,), (1,)), ((), ())), preferred_element_type=F32
            )
        return carry

    def weight_step(row, carry):
        score = jnp.where(lane < lengths_ref[0, row], scores_ref[row] * scale, -1e30)
        new_key = to_heads(newest_ref[row, :key_heads])
        new_value = to_heads(newest_ref[row, key_heads:])
        new_score = jnp.sum(query_heads_ref[row] * new_key, axis=1, keepdims=True) * scale
        top = jnp.maximum(jnp.max(score, axis=1, keepdims=True), new_score)
        weights = jnp.exp(score - top)
        new_weight = jnp.exp(new_score - top)
        denominator = jnp.sum(weights, axis=1, keepdims=True) + new_weight
        weights_ref[row] = (weights / denominator).astype(BF16)
        fresh_ref[row] = (new_weight / denominator).astype(BF16).astype(F32) * new_value
        return carry

    def value_step(row, carry):
        for k in range(0, key_heads, 2):
            values = cache_ref[1, row, :, k * HEAD_WIDTH : (k + 2) * HEAD_WIDTH]
            both = dot(weights_ref[row, k * groups : (k + 2) * groups], values)
            query_heads_ref[row, k * groups : (k + 1) * groups] = (
                both[:groups, :HEAD_WIDTH] + fresh_ref[row, k * groups : (k + 1) * groups]
            )
            query_heads_ref[row, (k + 1) * groups : (k + 2) * groups] = (
                both[groups:, HEAD_WIDTH:] + fresh_ref[row, (k + 1) * groups : (k + 2) * groups]
            )
        return carry

    for i in range(parts):
        copies[0][i].wait()
        for row in range(i * step, (i + 1) * step):
            score_step(row, 0)
        for row in range(i * step, (i + 1) * step):
            weight_step(row, 0)
    for i in range(parts):
        copies[1][i].wait()
        for row in range(i * step, (i + 1) * step):
            value_step(row, 0)
    for head in range(heads):
        out_ref[:, head * HEAD_WIDTH : (head + 1) * HEAD_WIDTH] = query_heads_ref[:, head, :].astype(BF16)


def attend(query_rows, newest_heads, cosine, sine, cache, lengths):
    tensor, own_rows, columns = query_rows.shape
    heads = tensor * columns // HEAD_WIDTH
    return pl.pallas_call(
        attend_kernel,
        in_specs=[SMEM] + [VMEM] * 4 + [HBM],
        out_specs=VMEM,
        out_shape=jax.ShapeDtypeStruct((own_rows, tensor * columns), BF16),
        scratch_shapes=[
            pltpu.VMEM((own_rows, heads, HEAD_WIDTH), F32),
            pltpu.VMEM((own_rows, heads, cache.shape[2]), F32),
            pltpu.VMEM((own_rows, heads, cache.shape[2]), BF16),
            pltpu.VMEM((own_rows, heads, HEAD_WIDTH), F32),
            pltpu.VMEM((2, own_rows) + cache.shape[2:], BF16),
            pltpu.SemaphoreType.DMA((2, 2)),
        ],
        compiler_params=params(),
        cost_estimate=pl.CostEstimate(flops=400000000, bytes_accessed=7000000, transcendentals=100000),
        name="attention",
    )(lengths, query_rows, newest_heads, cosine, sine, in_hbm(cache))


def make_body(mesh):
    tensor = mesh.shape["tensor"]
    shards = mesh.shape["adapter"]
    order = ring_order(tensor)
    place_of = [order.index(t) for t in range(tensor)]
    right = [(order[i], order[(i + 1) % tensor]) for i in range(tensor)]
    left = [(b, a) for a, b in right]
    swap = [(i, shards - 1 - i) for i in range(shards)]

    def table(own_adapters):
        lines = []
        for side in range(shards):
            for position in range(tensor):
                place = place_of[position]
                steps = [0] + [sign * step for step in range(1, tensor // 2) for sign in (-1, 1)] + [tensor // 2]
                owners = [order[(place + step) % tensor] for step in steps]
                lines.append([side * own_adapters, (shards - 1 - side) * own_adapters, position] + owners)
        return np.array(lines, np.int32)

    def everyone(x):
        return lax.all_to_all(x, "tensor", 0, 0, tiled=True)

    def go(x, pairs):
        return lax.ppermute(x, "tensor", pairs)

    def body(
        hidden,
        input_norm_scale,
        query_weight,
        key_value_weight,
        adapter_down_weight,
        adapter_up_query,
        adapter_up_key_value,
        request_adapter,
        key_value_cache,
        lengths,
    ):
        position = lax.axis_index("tensor")
        side = lax.axis_index("adapter")
        rows, width = hidden.shape[1:]
        own_rows = rows // tensor
        half = rows // 2
        own_adapters = adapter_down_weight.shape[0]
        rank = adapter_up_query.shape[1]
        kv_width = adapter_up_key_value.shape[3]
        gains = input_norm_scale.reshape(tensor, 1, width)
        labels = jnp.arange(shards * own_adapters, dtype=jnp.int32)
        first_rows = jnp.sum((request_adapter < labels[:, None]).astype(jnp.int32), axis=1)
        scalars = jnp.concatenate(
            [
                lax.dynamic_slice_in_dim(jnp.asarray(table(own_adapters)), side * tensor + position, 1, 0),
                first_rows[None],
            ],
            axis=1,
        )
        own_down = adapter_down_weight.transpose(0, 2, 1)
        cosine, sine = rotary_tables(lengths[0])

        local = (hidden[0, :half], hidden[0, half:])
        from_left = from_right = local
        blocks = []
        sums = None
        fresh_blocks = [local]
        for step in range(1, tensor // 2):
            top_left = go(from_left[0], right)
            bottom_right = go(from_right[1], left)
            top_right = go(from_right[0], left)
            bottom_left = go(from_left[1], right)
            from_left, from_right = (top_left, bottom_left), (top_right, bottom_right)
            if step == tensor // 2 - 1:
                sums = square_sums(fresh_blocks, sums)
                fresh_blocks = []
            blocks += [from_left, from_right]
            fresh_blocks += [from_left, from_right]
        last = (go(from_left[0], right), go(from_right[1], left))
        panels = (own_down, adapter_up_query, adapter_up_key_value)

        other_down, other_up, other_kv = (lax.ppermute(w, "adapter", swap) for w in panels)
        sums = square_sums(fresh_blocks, sums)
        blocks.append(last)

        inverse, keep, shrink, *gives = prep(
            scalars, sums, last, local, gains, key_value_weight, own_down, other_down, rank, tensor
        )
        gives = [give.astype(NARROW) for give in gives]
        shrink_parts = everyone(after(shrink, *gives))
        acc = query_products(scalars, 3, hidden[0], blocks, gains, query_weight, inverse)
        got = [
            go(give, [(t, t ^ (2 * d)) for t in range(tensor)]) for d, give in enumerate(gives, 1)
        ]
        mine, give = line_sums(scalars, keep, [part.astype(F32) for part in got])
        kv_parts = [mine, go(give.astype(NARROW), [(t, t ^ 1) for t in range(tensor)]).astype(F32)]
        query, kv_delta = finish(
            scalars, shrink_parts, (adapter_up_query, other_up), (adapter_up_key_value, other_kv), acc, rank
        )
        query_rows = everyone(after(query, *got).reshape(tensor, own_rows, -1))
        newest, newest_heads = fresh(kv_parts, kv_delta, cosine, sine)
        attended = attend(query_rows, newest_heads, cosine, sine, key_value_cache[0], lengths)
        return attended[None], newest[None]

    return body


def solution(mesh):
    return jax.shard_map(
        make_body(mesh),
        mesh=mesh,
        in_specs=(
            P("adapter", "group", "tensor"),
            P(),
            P(None, "tensor"),
            P("tensor", None),
            P(("group", "adapter"), "tensor", None),
            P(("group", "adapter"), None, "tensor"),
            P(("group", "adapter"), None, None, None),
            P("adapter", "group"),
            P("adapter", ("group", "tensor"), None, None, None),
            P("adapter", ("group", "tensor")),
        ),
        out_specs=(
            P("adapter", ("group", "tensor"), None),
            P("adapter", ("group", "tensor"), None, None),
        ),
        check_vma=False,
    )
```

```python
import functools
import math

import jax
import jax.numpy as jnp
import numpy as np
from jax import lax
from jax.experimental import pallas as pl
from jax.experimental.pallas import tpu as pltpu
from jax.sharding import PartitionSpec as P

HEAD_WIDTH = 128
LANES = 128
EPS = 1e-05
THETA = 500000.0
UNROLL = 4
NARROW = jnp.float16
SLOTS = 4
F32 = jnp.float32
BF16 = jnp.bfloat16


def ring_order(size):
    if size == 8:
        return [0, 2, 4, 6, 7, 5, 3, 1]
    return list(range(size))


def dot(a, b):
    return jnp.dot(a, b, preferred_element_type=F32)


def params(mib=16):
    return pltpu.CompilerParams(vmem_limit_bytes=mib * 1024 * 1024)


def after(value, *others):
    return lax.optimization_barrier((value, *others))[0]


VMEM = pl.BlockSpec(memory_space=pltpu.VMEM)
SMEM = pl.BlockSpec(memory_space=pltpu.SMEM)
HBM = pl.BlockSpec(memory_space=pltpu.HBM)


def in_hbm(value):
    return pltpu.with_memory_space_constraint(value, pltpu.HBM)


def rotary_tables(positions):
    half = HEAD_WIDTH // 2
    frequency = THETA ** (-(jnp.arange(half).astype(F32) * 2.0 / HEAD_WIDTH))
    angles = positions.astype(F32)[:, None] * frequency[None, :]
    cosine = jnp.cos(angles)
    sine = jnp.sin(angles)
    return jnp.concatenate([cosine, cosine], axis=1), jnp.concatenate([-sine, sine], axis=1)


def rotate_heads(values, cosine, sine):
    turned = []
    for head in range(values.shape[1] // HEAD_WIDTH):
        part = values[:, head * HEAD_WIDTH : (head + 1) * HEAD_WIDTH]
        turned.append(part * cosine + pltpu.roll(part, HEAD_WIDTH // 2, 1) * sine)
    return jnp.concatenate(turned, axis=1)


def pack_rows(values):
    most = jnp.max(jnp.abs(values), axis=1, keepdims=True)
    exponent = jnp.ceil(jnp.log2(jnp.maximum(most, 1e-30)))
    scaled = values * jnp.exp2(14.0 - exponent)
    return jnp.concatenate([scaled, jnp.broadcast_to(exponent, (values.shape[0], LANES))], axis=1)


def unpack_rows(values):
    width = values.shape[1] - LANES
    return values[:, :width] * jnp.exp2(values[:, width : width + 1] - 14.0)


def lane_sums(block):
    wide = block.astype(F32)
    squares = wide * wide
    lanes = squares[:, :LANES]
    for at in range(LANES, squares.shape[1], LANES):
        lanes = lanes + squares[:, at : at + LANES]
    return lanes


def sums_kernel(first, *refs):
    out_ref = refs[-1]
    half = out_ref.shape[0] // 2
    tops = refs[0:-1:2] if first else refs[0:-2:2]
    bottoms = refs[1:-1:2] if first else refs[1:-2:2]
    top = None if first else refs[-2][:half]
    bottom = None if first else refs[-2][half:]
    for top_ref, bottom_ref in zip(tops, bottoms):
        more, below = lane_sums(top_ref[...]), lane_sums(bottom_ref[...])
        top = more if top is None else top + more
        bottom = below if bottom is None else bottom + below
    out_ref[:half] = top
    out_ref[half:] = bottom


def square_sums(blocks, before):
    flat = [half for block in blocks for half in block]
    rows = 2 * flat[0].shape[0]
    operands = flat + ([] if before is None else [before])
    return pl.pallas_call(
        functools.partial(sums_kernel, before is None),
        in_specs=[VMEM] * len(operands),
        out_specs=VMEM,
        out_shape=jax.ShapeDtypeStruct((rows, LANES), F32),
        compiler_params=params(),
        cost_estimate=pl.CostEstimate(flops=1000000, bytes_accessed=600000, transcendentals=0),
        name="square_sums",
    )(*operands)


def id_column(scalar_ref, at, count, start, rows):
    row = start + lax.broadcasted_iota(jnp.int32, (rows, LANES), 0)
    ids = jnp.zeros((rows, LANES), jnp.int32)
    for label in range(1, count):
        ids = ids + jnp.where(row >= scalar_ref[0, at + label], 1, 0)
    return ids[:, :1]


def prep_kernel(
    rank, scalar_ref, sums_ref, last_top_ref, last_bottom_ref, top_ref, bottom_ref, other_ref,
    gain_hbm, own_hbm, weight_hbm, inverse_ref, keep_ref, shrink_ref, *refs,
):
    give_refs = refs[:-5]
    kv_ref, gain_ref, own_ref, weight_ref, sems = refs[-5:]
    rows, width = inverse_ref.shape[0], top_ref.shape[1]
    model_width = gain_hbm.shape[0] * width
    chunks = sems.shape[0] - 2
    depth = width // chunks
    first = [
        pltpu.make_async_copy(gain_hbm.at[scalar_ref[0, 2]], gain_ref, sems.at[chunks]),
        pltpu.make_async_copy(own_hbm, own_ref, sems.at[chunks + 1]),
    ]
    copies = [
        pltpu.make_async_copy(
            weight_hbm.at[pl.ds(c * depth, depth)], weight_ref.at[pl.ds(c * depth, depth)], sems.at[c]
        )
        for c in range(chunks)
    ]
    for copy in first + copies:
        copy.start()
    last = jnp.concatenate([lane_sums(last_top_ref[...]), lane_sums(last_bottom_ref[...])], axis=0)
    total = jnp.sum((sums_ref[...] + last).T, axis=0, keepdims=True)
    inverse_row = lax.rsqrt(total / model_width + EPS)
    inverse = jnp.broadcast_to(inverse_row, (LANES, rows)).T
    inverse_ref[...] = inverse
    adapters = 2 * own_ref.shape[0]
    ids = id_column(scalar_ref, 3 + gain_hbm.shape[0], adapters, 0, rows)
    first[0].wait()
    block = jnp.concatenate([top_ref[...], bottom_ref[...]], axis=0).astype(F32)
    normed = (block * inverse[:, :1] * gain_ref[...]).astype(BF16)
    first[1].wait()
    shrink = jnp.zeros((rows, 3 * rank), F32)
    for side, panel_ref in enumerate((own_ref, other_ref)):
        for j in range(panel_ref.shape[0]):
            part = lax.dot_general(normed, panel_ref[j], (((1,), (1,)), ((), ())), preferred_element_type=F32)
            shrink = shrink + jnp.where(ids == scalar_ref[0, side] + j, part, 0.0)
    half = rows // 2
    packed = jnp.concatenate([shrink[:half, :rank], shrink[half:, :rank]], axis=1)
    tensor, page, _ = shrink_ref.shape
    own_rows = page - half
    for peer in range(tensor):
        shrink_ref[peer, :half] = packed
        shrink_ref[peer, half:] = shrink[peer * own_rows : (peer + 1) * own_rows, rank:]
    total = None
    for c, copy in enumerate(copies):
        copy.wait()
        part = dot(normed[:, c * depth : (c + 1) * depth], weight_ref[c * depth : (c + 1) * depth])
        total = part if total is None else total + part
    kv_ref[...] = total
    index = lax.div(scalar_ref[0, 2], 2)
    both = 2 * own_rows
    keep_ref[...] = kv_ref[pl.ds(pl.multiple_of(index * both, both), both)]
    for distance, give_ref in enumerate(give_refs, 1):
        give_ref[...] = pack_rows(kv_ref[pl.ds(pl.multiple_of((index ^ distance) * both, both), both)])


def prep(scalars, sums, last, local, gains, weight, own, other, rank, tensor):
    half, width = local[0].shape
    rows = 2 * half
    columns = weight.shape[1]
    chunks = 4 if width % 1024 == 0 else 1
    page = rows // 2 + rows // tensor
    return pl.pallas_call(
        functools.partial(prep_kernel, rank),
        in_specs=[SMEM] + [VMEM] * 6 + [HBM] * 3,
        out_specs=[VMEM] * (tensor // 2 + 2),
        out_shape=[
            pltpu.HBM((rows, LANES), F32),
            pltpu.HBM((2 * rows // tensor, columns), F32),
            pltpu.HBM((tensor, page, LANES), F32),
        ]
        + [jax.ShapeDtypeStruct((2 * rows // tensor, columns + LANES), F32)] * (tensor // 2 - 1),
        scratch_shapes=[
            pltpu.VMEM((rows, columns), F32),
            pltpu.VMEM((1, width), F32),
            pltpu.VMEM(own.shape, BF16),
            pltpu.VMEM(weight.shape, BF16),
            pltpu.SemaphoreType.DMA((chunks + 2,)),
        ],
        compiler_params=params(),
        cost_estimate=pl.CostEstimate(flops=700000000, bytes_accessed=6000000, transcendentals=0),
        name="norm_key_value_shrink",
    )(scalars, sums, *last, *local, other, in_hbm(gains), in_hbm(own), in_hbm(weight))


def query_kernel(columns_at, scalar_ref, *refs):
    blocks = refs[:-10]
    hidden_hbm, inverse_hbm, gain_hbm, weight_hbm, out_ref, own_ref, inverse_ref, gain_ref, weight_ref, sems = refs[-10:]
    count = 1 + len(blocks) // 2
    width = own_ref.shape[1]
    slots = weight_ref.shape[0]
    order = list(range(1, count)) + [0]

    def owner(i):
        return scalar_ref[0, columns_at + order[i]]

    def fetch(i):
        return pltpu.make_async_copy(
            weight_hbm.at[pl.ds(pl.multiple_of(owner(i) * width, width), width)],
            weight_ref.at[i % slots],
            sems.at[i % slots],
        )

    small = [
        pltpu.make_async_copy(inverse_hbm, inverse_ref, sems.at[slots]),
        pltpu.make_async_copy(gain_hbm, gain_ref, sems.at[slots + 1]),
        pltpu.make_async_copy(hidden_hbm, own_ref, sems.at[slots + 2]),
    ]
    for copy in small[:2]:
        copy.start()
    for i in range(min(slots, count)):
        fetch(i).start()
    small[2].start()
    for copy in small[:2]:
        copy.wait()
    inverse = inverse_ref[:, :1]
    for i in range(count):
        gain = gain_ref[pl.ds(owner(i), 1)].reshape(1, width)
        if order[i] == 0:
            small[2].wait()
            block = own_ref[...].astype(F32)
        else:
            at = 2 * order[i] - 2
            block = jnp.concatenate([blocks[at][...], blocks[at + 1][...]], axis=0).astype(F32)
        normed = (block * inverse * gain).astype(BF16)
        fetch(i).wait()
        part = dot(normed, weight_ref[i % slots])
        out_ref[...] = part if i == 0 else out_ref[...] + part
        if i + slots < count:
            fetch(i + slots).start()


def query_products(scalars, columns_at, hidden, blocks, gains, weight, inverse):
    rows, width = hidden.shape
    columns = weight.shape[1]
    count = 1 + len(blocks)
    flat = [half for block in blocks for half in block]
    slots = min(SLOTS, count)
    return pl.pallas_call(
        functools.partial(query_kernel, columns_at),
        in_specs=[SMEM] + [VMEM] * len(flat) + [HBM] * 4,
        out_specs=VMEM,
        out_shape=jax.ShapeDtypeStruct((rows, columns), F32),
        scratch_shapes=[
            pltpu.VMEM(hidden.shape, BF16),
            pltpu.VMEM(inverse.shape, F32),
            pltpu.VMEM(gains.shape, F32),
            pltpu.VMEM((slots, width, columns), BF16),
            pltpu.SemaphoreType.DMA((slots + 3,)),
        ],
        compiler_params=params(24),
        cost_estimate=pl.CostEstimate(flops=2000000000, bytes_accessed=17000000, transcendentals=0),
        name="query_products",
    )(scalars, *flat, in_hbm(hidden), in_hbm(inverse), in_hbm(gains), in_hbm(weight))


def spread(ids, values, first, second, each):
    labels = [first + j for j in range(each)] + [second + j for j in range(each)]
    return jnp.concatenate([jnp.where(ids == label, values, 0.0) for label in labels], axis=1).astype(BF16)


def finish_kernel(
    rank, scalar_ref, parts_ref, acc_ref, up_other_ref, up_own_hbm, kv_own_hbm, kv_other_hbm,
    out_ref, kv_delta_ref, up_ref, kv_ref, sems,
):
    each = up_own_hbm.shape[0]
    copies = [
        pltpu.make_async_copy(up_own_hbm, up_ref, sems.at[0]),
        pltpu.make_async_copy(kv_own_hbm, kv_ref.at[pl.ds(0, each)], sems.at[1]),
        pltpu.make_async_copy(kv_other_hbm, kv_ref.at[pl.ds(each, each)], sems.at[2]),
    ]
    for copy in copies:
        copy.start()
    rows = out_ref.shape[0]
    half = rows // 2
    own_rows, kv_columns = kv_delta_ref.shape
    kv_width = kv_columns // 2
    columns = out_ref.shape[1]
    first, second = scalar_ref[0, 0], scalar_ref[0, 1]
    at = 3 + parts_ref.shape[0]
    ids = id_column(scalar_ref, at, 2 * each, 0, rows)
    own_ids = id_column(scalar_ref, at, 2 * each, scalar_ref[0, 2] * own_rows, own_rows)
    total = parts_ref[0]
    for peer in range(1, parts_ref.shape[0]):
        total = total + parts_ref[peer]
    shrink = jnp.concatenate([total[:half, :rank], total[:half, rank:]], axis=0)
    query_spread = spread(ids, shrink, first, second, each)
    key_spread = spread(own_ids, total[half:, :rank], first, second, each)
    value_spread = spread(own_ids, total[half:, rank:], first, second, each)
    depth = 2 * each * rank
    other_part = dot(query_spread[:, depth // 2 :], up_other_ref[...].reshape(depth // 2, columns))
    copies[0].wait()
    own_part = dot(query_spread[:, : depth // 2], up_ref[...].reshape(depth // 2, columns))
    out_ref[...] = (acc_ref[...] + own_part + other_part).astype(BF16)
    copies[1].wait()
    copies[2].wait()
    kv_delta_ref[:, :kv_width] = dot(key_spread, kv_ref[:, 0].reshape(depth, kv_width))
    kv_delta_ref[:, kv_width:] = dot(value_spread, kv_ref[:, 1].reshape(depth, kv_width))


def finish(scalars, parts, ups, kv_ups, acc, rank):
    rows = acc.shape[0]
    own_rows = rows // parts.shape[0]
    columns = ups[0].shape[2]
    kv_columns = 2 * kv_ups[0].shape[3]
    each = ups[0].shape[0]
    return pl.pallas_call(
        functools.partial(finish_kernel, rank),
        in_specs=[SMEM] + [VMEM] * 3 + [HBM] * 3,
        out_specs=[VMEM, VMEM],
        out_shape=[
            jax.ShapeDtypeStruct((rows, columns), BF16),
            jax.ShapeDtypeStruct((own_rows, kv_columns), F32),
        ],
        scratch_shapes=[
            pltpu.VMEM(ups[0].shape, BF16),
            pltpu.VMEM((2 * each,) + kv_ups[0].shape[1:], BF16),
            pltpu.SemaphoreType.DMA((3,)),
        ],
        compiler_params=params(),
        cost_estimate=pl.CostEstimate(flops=100000000, bytes_accessed=2000000, transcendentals=0),
        name="adapter_terms",
    )(scalars, parts, acc, ups[1], in_hbm(ups[0]), in_hbm(kv_ups[0]), in_hbm(kv_ups[1]))


def line_kernel(scalar_ref, keep_ref, *refs):
    got_refs, (mine_ref, give_ref, total_ref) = refs[:-3], refs[-3:]
    own_rows = mine_ref.shape[0]
    total = keep_ref[...]
    for got_ref in got_refs:
        total = total + unpack_rows(got_ref[...])
    total_ref[...] = total
    parity = scalar_ref[0, 2] % 2
    mine_ref[...] = total_ref[pl.ds(pl.multiple_of(parity * own_rows, own_rows), own_rows)]
    give_ref[...] = pack_rows(total_ref[pl.ds(pl.multiple_of((1 - parity) * own_rows, own_rows), own_rows)])


def line_sums(scalars, keep, got):
    both, columns = keep.shape
    return pl.pallas_call(
        line_kernel,
        in_specs=[SMEM] + [VMEM] * (1 + len(got)),
        out_specs=[VMEM] * 2,
        out_shape=[
            jax.ShapeDtypeStruct((both // 2, columns), F32),
            jax.ShapeDtypeStruct((both // 2, columns + LANES), F32),
        ],
        scratch_shapes=[pltpu.VMEM(keep.shape, F32)],
        compiler_params=params(),
        cost_estimate=pl.CostEstimate(flops=100000, bytes_accessed=1500000, transcendentals=0),
        name="line_sums",
    )(scalars, in_hbm(keep), *got)


def fresh_kernel(count, *refs):
    parts = refs[:count]
    delta_ref, cosine_ref, sine_ref, out_ref, heads_ref = refs[count:]
    total = parts[0][...]
    for part in parts[1:]:
        total = total + unpack_rows(part[...])
    total = total + delta_ref[...]
    kv_width = total.shape[1] // 2
    newest = jnp.concatenate(
        [rotate_heads(total[:, :kv_width], cosine_ref[...], sine_ref[...]), total[:, kv_width:]], axis=1
    ).astype(BF16)
    out_ref[:, 0, :] = newest[:, :kv_width]
    out_ref[:, 1, :] = newest[:, kv_width:]
    spread = newest.astype(F32)
    for head in range(heads_ref.shape[1]):
        heads_ref[:, head, :] = spread[:, head * HEAD_WIDTH : (head + 1) * HEAD_WIDTH]


def fresh(parts, delta, cosine, sine):
    own_rows, columns = delta.shape
    return pl.pallas_call(
        functools.partial(fresh_kernel, len(parts)),
        out_shape=[
            jax.ShapeDtypeStruct((own_rows, 2, columns // 2), BF16),
            jax.ShapeDtypeStruct((own_rows, columns // HEAD_WIDTH, HEAD_WIDTH), F32),
        ],
        compiler_params=params(),
        cost_estimate=pl.CostEstimate(flops=100000, bytes_accessed=1000000, transcendentals=0),
        name="new_key_value",
    )(*parts, delta, cosine, sine)


def attend_kernel(
    lengths_ref, query_ref, newest_ref, cosine_ref, sine_ref, cache_hbm, out_ref, query_heads_ref, scores_ref, weights_ref, fresh_ref,
    cache_ref, sems,
):
    tensor, own_rows, columns = query_ref.shape
    per_peer = columns // HEAD_WIDTH
    positions = cache_ref.shape[2]
    key_heads = cache_ref.shape[3] // HEAD_WIDTH
    heads = tensor * per_peer
    groups = heads // key_heads
    scale = 1.0 / math.sqrt(HEAD_WIDTH)
    pair = 2 * groups
    parts = sems.shape[1]
    step = own_rows // parts
    copies = [
        [
            pltpu.make_async_copy(
                cache_hbm.at[pl.ds(i * step, step), which], cache_ref.at[which, pl.ds(i * step, step)], sems.at[which, i]
            )
            for i in range(parts)
        ]
        for which in range(2)
    ]
    for copy in copies[0] + copies[1]:
        copy.start()
    for peer in range(tensor):
        part = rotate_heads(query_ref[peer].astype(F32), cosine_ref[...], sine_ref[...]).astype(BF16).astype(F32)
        for j in range(per_peer):
            query_heads_ref[:, peer * per_peer + j, :] = part[:, j * HEAD_WIDTH : (j + 1) * HEAD_WIDTH]
    side = lax.broadcasted_iota(jnp.int32, (pair, 2 * HEAD_WIDTH), 0) < groups
    on_side = side == (lax.broadcasted_iota(jnp.int32, (pair, 2 * HEAD_WIDTH), 1) < HEAD_WIDTH)
    lane = lax.broadcasted_iota(jnp.int32, (heads, positions), 1)

    def to_heads(part):
        return jnp.broadcast_to(part[:, None, :], (key_heads, groups, HEAD_WIDTH)).reshape(heads, HEAD_WIDTH)

    def score_step(row, carry):
        query = query_heads_ref[row]
        for k in range(0, key_heads, 2):
            two = query[k * groups : (k + 2) * groups]
            spread = jnp.where(on_side, jnp.concatenate([two, two], axis=1), 0.0).astype(BF16)
            keys = cache_ref[0, row, :, k * HEAD_WIDTH : (k + 2) * HEAD_WIDTH]
            scores_ref[row, k * groups : (k + 2) * groups] = lax.dot_general(
                spread, keys, (((1,), (1,)), ((), ())), preferred_element_type=F32
            )
        return carry

    def weight_step(row, carry):
        score = jnp.where(lane < lengths_ref[0, row], scores_ref[row] * scale, -1e30)
        new_key = to_heads(newest_ref[row, :key_heads])
        new_value = to_heads(newest_ref[row, key_heads:])
        new_score = jnp.sum(query_heads_ref[row] * new_key, axis=1, keepdims=True) * scale
        top = jnp.maximum(jnp.max(score, axis=1, keepdims=True), new_score)
        weights = jnp.exp(score - top)
        new_weight = jnp.exp(new_score - top)
        denominator = jnp.sum(weights, axis=1, keepdims=True) + new_weight
        weights_ref[row] = (weights / denominator).astype(BF16)
        fresh_ref[row] = (new_weight / denominator).astype(BF16).astype(F32) * new_value
        return carry

    def value_step(row, carry):
        for k in range(0, key_heads, 2):
            values = cache_ref[1, row, :, k * HEAD_WIDTH : (k + 2) * HEAD_WIDTH]
            both = dot(weights_ref[row, k * groups : (k + 2) * groups], values)
            query_heads_ref[row, k * groups : (k + 1) * groups] = (
                both[:groups, :HEAD_WIDTH] + fresh_ref[row, k * groups : (k + 1) * groups]
            )
            query_heads_ref[row, (k + 1) * groups : (k + 2) * groups] = (
                both[groups:, HEAD_WIDTH:] + fresh_ref[row, (k + 1) * groups : (k + 2) * groups]
            )
        return carry

    for i in range(parts):
        copies[0][i].wait()
        for row in range(i * step, (i + 1) * step):
            score_step(row, 0)
        for row in range(i * step, (i + 1) * step):
            weight_step(row, 0)
    for i in range(parts):
        copies[1][i].wait()
        for row in range(i * step, (i + 1) * step):
            value_step(row, 0)
    for head in range(heads):
        out_ref[:, head * HEAD_WIDTH : (head + 1) * HEAD_WIDTH] = query_heads_ref[:, head, :].astype(BF16)


def attend(query_rows, newest_heads, cosine, sine, cache, lengths):
    tensor, own_rows, columns = query_rows.shape
    heads = tensor * columns // HEAD_WIDTH
    return pl.pallas_call(
        attend_kernel,
        in_specs=[SMEM] + [VMEM] * 4 + [HBM],
        out_specs=VMEM,
        out_shape=jax.ShapeDtypeStruct((own_rows, tensor * columns), BF16),
        scratch_shapes=[
            pltpu.VMEM((own_rows, heads, HEAD_WIDTH), F32),
            pltpu.VMEM((own_rows, heads, cache.shape[2]), F32),
            pltpu.VMEM((own_rows, heads, cache.shape[2]), BF16),
            pltpu.VMEM((own_rows, heads, HEAD_WIDTH), F32),
            pltpu.VMEM((2, own_rows) + cache.shape[2:], BF16),
            pltpu.SemaphoreType.DMA((2, 2)),
        ],
        compiler_params=params(),
        cost_estimate=pl.CostEstimate(flops=400000000, bytes_accessed=7000000, transcendentals=100000),
        name="attention",
    )(lengths, query_rows, newest_heads, cosine, sine, in_hbm(cache))


def make_body(mesh):
    tensor = mesh.shape["tensor"]
    shards = mesh.shape["adapter"]
    order = ring_order(tensor)
    place_of = [order.index(t) for t in range(tensor)]
    right = [(order[i], order[(i + 1) % tensor]) for i in range(tensor)]
    left = [(b, a) for a, b in right]
    swap = [(i, shards - 1 - i) for i in range(shards)]

    def table(own_adapters):
        lines = []
        for side in range(shards):
            for position in range(tensor):
                place = place_of[position]
                steps = [0] + [sign * step for step in range(1, tensor // 2) for sign in (-1, 1)] + [tensor // 2]
                owners = [order[(place + step) % tensor] for step in steps]
                lines.append([side * own_adapters, (shards - 1 - side) * own_adapters, position] + owners)
        return np.array(lines, np.int32)

    def everyone(x):
        return lax.all_to_all(x, "tensor", 0, 0, tiled=True)

    def go(x, pairs):
        return lax.ppermute(x, "tensor", pairs)

    def body(
        hidden,
        input_norm_scale,
        query_weight,
        key_value_weight,
        adapter_down_weight,
        adapter_up_query,
        adapter_up_key_value,
        request_adapter,
        key_value_cache,
        lengths,
    ):
        position = lax.axis_index("tensor")
        side = lax.axis_index("adapter")
        rows, width = hidden.shape[1:]
        own_rows = rows // tensor
        half = rows // 2
        own_adapters = adapter_down_weight.shape[0]
        rank = adapter_up_query.shape[1]
        kv_width = adapter_up_key_value.shape[3]
        gains = input_norm_scale.reshape(tensor, 1, width)
        labels = jnp.arange(shards * own_adapters, dtype=jnp.int32)
        first_rows = jnp.sum((request_adapter < labels[:, None]).astype(jnp.int32), axis=1)
        scalars = jnp.concatenate(
            [
                lax.dynamic_slice_in_dim(jnp.asarray(table(own_adapters)), side * tensor + position, 1, 0),
                first_rows[None],
            ],
            axis=1,
        )
        own_down = adapter_down_weight.transpose(0, 2, 1)
        cosine, sine = rotary_tables(lengths[0])

        local = (hidden[0, :half], hidden[0, half:])
        from_left = from_right = local
        blocks = []
        sums = None
        fresh_blocks = [local]
        for step in range(1, tensor // 2):
            top_left = go(from_left[0], right)
            bottom_right = go(from_right[1], left)
            top_right = go(from_right[0], left)
            bottom_left = go(from_left[1], right)
            from_left, from_right = (top_left, bottom_left), (top_right, bottom_right)
            if step == tensor // 2 - 1:
                sums = square_sums(fresh_blocks, sums)
                fresh_blocks = []
            blocks += [from_left, from_right]
            fresh_blocks += [from_left, from_right]
        last = (go(from_left[0], right), go(from_right[1], left))
        panels = (own_down, adapter_up_query, adapter_up_key_value)

        other_down, other_up, other_kv = (lax.ppermute(w, "adapter", swap) for w in panels)
        sums = square_sums(fresh_blocks, sums)
        blocks.append(last)

        inverse, keep, shrink, *gives = prep(
            scalars, sums, last, local, gains, key_value_weight, own_down, other_down, rank, tensor
        )
        gives = [give.astype(NARROW) for give in gives]
        shrink_parts = everyone(after(shrink, *gives[1:]))
        acc = query_products(scalars, 3, hidden[0], blocks, gains, query_weight, inverse)
        got = [
            go(give, [(t, t ^ (2 * d)) for t in range(tensor)]) for d, give in enumerate(gives, 1)
        ]
        mine, give = line_sums(scalars, keep, [part.astype(F32) for part in got])
        kv_parts = [mine, go(give.astype(NARROW), [(t, t ^ 1) for t in range(tensor)]).astype(F32)]
        query, kv_delta = finish(
            scalars, shrink_parts, (adapter_up_query, other_up), (adapter_up_key_value, other_kv), acc, rank
        )
        query_rows = everyone(after(query, *got).reshape(tensor, own_rows, -1))
        newest, newest_heads = fresh(kv_parts, kv_delta, cosine, sine)
        attended = attend(query_rows, newest_heads, cosine, sine, key_value_cache[0], lengths)
        return attended[None], newest[None]

    return body


def solution(mesh):
    return jax.shard_map(
        make_body(mesh),
        mesh=mesh,
        in_specs=(
            P("adapter", "group", "tensor"),
            P(),
            P(None, "tensor"),
            P("tensor", None),
            P(("group", "adapter"), "tensor", None),
            P(("group", "adapter"), None, "tensor"),
            P(("group", "adapter"), None, None, None),
            P("adapter", "group"),
            P("adapter", ("group", "tensor"), None, None, None),
            P("adapter", ("group", "tensor")),
        ),
        out_specs=(
            P("adapter", ("group", "tensor"), None),
            P("adapter", ("group", "tensor"), None, None),
        ),
        check_vma=False,
    )
```
